32 devices in a mesh: pipe: 2 (over core), dp: 16 (over z, y, x).
Axes of the slice: x: 2, y: 2, z: 4, core: 2. Of those that a mesh axis runs over, the one named last changes fastest.
Arguments:
- images: bfloat16 [2, 16, 196, 216], P(None, 'dp'), may hold values from -32 to 32
- codes: int32 [2, 4], replicated, may hold values from 0 to 2, as said below
- cotangent: bfloat16 [2, 16, 196, 216], P(None, 'dp'), may hold values from -5 to 5
- expand_weight: bfloat16 [216, 1296], replicated, may hold values from -0.4375 to 0.4375
- batch_gain: float32 [1296], replicated, may hold values from 0.5 to 1.5
- batch_bias: float32 [1296], replicated, may hold values from -3 to 3
- depth_one: float32 [9, 1296], replicated, may hold values from -2 to 2
- squeeze_weight: bfloat16 [1296, 324], replicated, may hold values from -0.3125 to 0.3125
- squeeze_bias: float32 [324], replicated, may hold values from -3 to 3
- excite_weight: bfloat16 [324, 1296], replicated, may hold values from -0.3125 to 0.3125
- excite_bias: float32 [1296], replicated, may hold values from -3 to 3
- project_weight: bfloat16 [1296, 216], replicated, may hold values from -0.3125 to 0.3125
- norm_gain: float32 [216], replicated, may hold values from 0.5 to 1.5
- norm_bias: float32 [216], replicated, may hold values from -2 to 2
- qkv_weight: bfloat16 [216, 648], replicated, may hold values from -0.4375 to 0.4375
- talk_before: float32 [12, 12], replicated, may hold values from -3 to 3
- talk_after: float32 [12, 12], replicated, may hold values from -3 to 3
- output_weight: bfloat16 [216, 216], replicated, may hold values from -3 to 3
- output_bias: float32 [216], replicated, may hold values from -2 to 2
- mlp_gain: float32 [216], replicated, may hold values from 0.5 to 1.5
- mlp_bias: float32 [216], replicated, may hold values from -2 to 2
- hidden_weight: bfloat16 [216, 864], replicated, may hold values from -0.4375 to 0.4375
- hidden_bias: float32 [864], replicated, may hold values from -2 to 2
- depth_two: float32 [9, 864], replicated, may hold values from -2 to 2
- return_weight: bfloat16 [864, 216], replicated, may hold values from -0.625 to 0.625
- return_bias: float32 [216], replicated, may hold values from -2 to 2
Outputs:
- activations: bfloat16 [2, 2, 16, 196, 216], P('pipe', None, 'dp')
- input_grads: float32 [2, 2, 16, 196, 216], P('pipe', None, 'dp')
- expand_weight_grad: float32 [216, 1296], replicated
- batch_gain_grad: float32 [1296], replicated
- batch_bias_grad: float32 [1296], replicated
- depth_one_grad: float32 [9, 1296], replicated
- squeeze_weight_grad: float32 [1296, 324], replicated
- squeeze_bias_grad: float32 [324], replicated
- excite_weight_grad: float32 [324, 1296], replicated
- excite_bias_grad: float32 [1296], replicated
- project_weight_grad: float32 [1296, 216], replicated
- norm_gain_grad: float32 [216], replicated
- norm_bias_grad: float32 [216], replicated
- qkv_weight_grad: float32 [216, 648], replicated
- talk_before_grad: float32 [12, 12], replicated
- talk_after_grad: float32 [12, 12], replicated
- output_weight_grad: float32 [216, 216], replicated
- output_bias_grad: float32 [216], replicated
- mlp_gain_grad: float32 [216], replicated
- mlp_bias_grad: float32 [216], replicated
- hidden_weight_grad: float32 [216, 864], replicated
- hidden_bias_grad: float32 [864], replicated
- depth_two_grad: float32 [9, 864], replicated
- return_weight_grad: float32 [864, 216], replicated
- return_bias_grad: float32 [216], replicated
The draws below stay inside these ranges and needn't reach their ends.
Inputs may be any that keep to these rules, and one draw needn't show every extreme that they name: `codes`: each of the four columns holds 2 in at least one micro-batch.
All inputs are finite; a program needn't handle non-finite values.
Results may differ from the reference program's by a relative error of at most 0.017.
The reference program's roundings to bfloat16 on the way count: a program that leaves them out, or rounds other values in their place, can miss the bound.
Values may be sent and summed in bfloat16 or wider, within the bound.
No kernel may reach another device: no remote copies, remote signals or barrier semaphores. Data moves between devices by JAX's collectives and lax.ppermute only.
A program may use at most 128 MiB of HBM per device.

```python
import jax
import jax.numpy as jnp
from jax import lax

D = 216
E = 1296
SQ = 324
HEADS = 12
HD = 18
F = 864
MICRO = 2
SIDE = 14
PIX = 196
IMGS = 16


def draw_images(key, part):
    key = jax.random.fold_in(key, 11)
    noise_key, scale_key, offset_key = jax.random.split(key, 3)
    noise_field = jax.random.truncated_normal(noise_key, -4.0, 4.0, (MICRO, IMGS, PIX, D), jnp.float32)
    reach_top = 3.0
    rising = reach_top ** (jnp.arange(IMGS).astype(jnp.float32) / (IMGS - 1))
    jitter = jax.random.uniform(scale_key, (MICRO, IMGS), jnp.float32, 0.8, 1.25)
    offset = jax.random.uniform(offset_key, (D,), jnp.float32, -1.0, 1.0)
    return ((noise_field + offset) * (rising * jitter)[:, :, None, None]).astype(jnp.bfloat16)


def draw_codes(key, part):
    key = jax.random.fold_in(key, 23)
    base_key, pick_key = jax.random.split(key)
    base_codes = jax.random.randint(base_key, (MICRO, 4), 0, 3)
    chosen = jax.random.randint(pick_key, (4,), 0, MICRO)
    row_index = jnp.arange(MICRO)[:, None]
    return jnp.where(row_index == chosen[None, :], 2, base_codes).astype(jnp.int32)


def level_of(own_key, dims, cuts, low, top_value):
    gain = 1.0
    for dim, shards_of in cuts:
        draws = jax.random.uniform(jax.random.fold_in(jax.random.fold_in(own_key, 6), dim), (shards_of,), jnp.float32, low / len(cuts), top_value / len(cuts))
        gain = gain * jnp.repeat(jnp.exp(draws), dims[dim] // shards_of).reshape((-1,) + (1,) * (len(dims) - 1 - dim))
    return gain


def gaussian(key, dims, scale, reach, shards=(), kind=jnp.bfloat16):
    values = scale * jax.random.normal(key, dims, jnp.float32)
    if shards:
        values = values * level_of(key, dims, shards, -0.22, 0.18)
    return jnp.clip(values, -reach, reach).astype(kind)


def setup_inputs(seed: int = 0) -> dict:
    key_list = jax.random.split(jax.random.key(seed), 27)
    images = draw_images(jax.random.fold_in(key_list[26], 71), 0)
    codes = draw_codes(jax.random.fold_in(key_list[26], 71), 0)
    cotangent = gaussian(key_list[2], (MICRO, IMGS, PIX, D), 1.0, 5.0, ((1, 16),))
    expand_weight = gaussian(key_list[3], (D, E), D ** -0.5, 0.4375)
    batch_gain = jnp.clip(1.0 + 0.1 * jax.random.normal(key_list[4], (E,), jnp.float32), 0.5, 1.5)
    batch_bias = gaussian(key_list[5], (E,), 0.5, 3.0, (), jnp.float32)
    depth_one = gaussian(key_list[6], (9, E), 9 ** -0.5, 2.0, (), jnp.float32)
    squeeze_weight = gaussian(key_list[7], (E, SQ), (E // 4) ** -0.5, 0.3125)
    squeeze_bias = gaussian(key_list[8], (SQ,), 0.5, 3.0, (), jnp.float32)
    excite_weight = gaussian(key_list[9], (SQ, E), SQ ** -0.5, 0.3125)
    excite_bias = gaussian(key_list[10], (E,), 0.5, 3.0, (), jnp.float32)
    project_weight = gaussian(key_list[11], (E, D), (E // 4) ** -0.5, 0.3125)
    norm_gain = jnp.clip(1.0 + 0.1 * jax.random.normal(key_list[12], (D,), jnp.float32), 0.5, 1.5)
    norm_bias = gaussian(key_list[13], (D,), 0.3, 2.0, (), jnp.float32)
    qkv_weight = gaussian(key_list[14], (D, 3 * D), D ** -0.5, 0.4375)
    talk_before = gaussian(key_list[15], (HEADS, HEADS), 0.5, 3.0, (), jnp.float32)
    talk_after = gaussian(key_list[16], (HEADS, HEADS), 0.5, 3.0, (), jnp.float32)
    output_weight = gaussian(key_list[17], (D, D), 4 ** -0.5, 3.0)
    output_bias = gaussian(key_list[18], (D,), 0.3, 2.0, (), jnp.float32)
    mlp_gain = jnp.clip(1.0 + 0.1 * jax.random.normal(key_list[19], (D,), jnp.float32), 0.5, 1.5)
    mlp_bias = gaussian(key_list[20], (D,), 0.3, 2.0, (), jnp.float32)
    hidden_weight = gaussian(key_list[21], (D, F), D ** -0.5, 0.4375)
    hidden_bias = gaussian(key_list[22], (F,), 0.3, 2.0, (), jnp.float32)
    depth_two = gaussian(key_list[23], (9, F), 9 ** -0.5, 2.0, (), jnp.float32)
    return_weight = gaussian(key_list[24], (F, D), (F // 8) ** -0.5, 0.625)
    return_bias = gaussian(key_list[25], (D,), 0.3, 2.0, (), jnp.float32)
    return {"images": images, "codes": codes, "cotangent": cotangent, "expand_weight": expand_weight, "batch_gain": batch_gain, "batch_bias": batch_bias, "depth_one": depth_one, "squeeze_weight": squeeze_weight, "squeeze_bias": squeeze_bias, "excite_weight": excite_weight, "excite_bias": excite_bias, "project_weight": project_weight, "norm_gain": norm_gain, "norm_bias": norm_bias, "qkv_weight": qkv_weight, "talk_before": talk_before, "talk_after": talk_after, "output_weight": output_weight, "output_bias": output_bias, "mlp_gain": mlp_gain, "mlp_bias": mlp_bias, "hidden_weight": hidden_weight, "hidden_bias": hidden_bias, "depth_two": depth_two, "return_weight": return_weight, "return_bias": return_bias}


highest = lax.Precision.HIGHEST
epsilon = 1e-05

@jax.custom_vjp
def low(v):
    return lax.optimization_barrier(v.astype(jnp.bfloat16)).astype(jnp.float32)

@jax.custom_vjp
def low_back(v):
    return v

def low_keep(v):
    return (low(v), None)

def low_pass(kept, grad):
    return (grad,)

def back_keep(v):
    return (v, None)

def back_low(kept, grad):
    return (low(grad),)
low.defvjp(low_keep, low_pass)
low_back.defvjp(back_keep, back_low)

def pixel_mask(image_side):
    positions = jnp.arange(SIDE * SIDE)
    inside = (positions // SIDE < image_side) & (positions % SIDE < image_side)
    return inside.astype(jnp.float32)

def code_masks(subnet_code):
    image_side = SIDE - 4 + 2 * subnet_code[3]
    pixels = pixel_mask(image_side)
    channel_mask = (jnp.arange(E) < E - (2 - subnet_code[0]) * D).astype(jnp.float32)
    head_mask = (jnp.arange(HEADS) < HEADS - 2 * (2 - subnet_code[1])).astype(jnp.float32)
    unit_mask = (jnp.arange(F) < F - (2 - subnet_code[2]) * D).astype(jnp.float32)
    return (image_side, pixels, channel_mask, head_mask, unit_mask)

def depthwise(fields, kernel):
    amount = fields.shape[0]
    channels = fields.shape[-1]
    squares = fields.reshape(amount, SIDE, SIDE, channels)
    padded = jnp.pad(squares, ((0, 0), (1, 1), (1, 1), (0, 0)))
    summed = jnp.zeros(squares.shape, fields.dtype)
    for vertical in range(3):
        for lateral in range(3):
            summed = summed + padded[:, vertical:vertical + SIDE, lateral:lateral + SIDE, :] * kernel[3 * vertical + lateral]
    return summed.reshape(amount, SIDE * SIDE, channels)

def layer_norm(values, gain_vector, bias_vector):
    centred = values - lax.optimization_barrier(jnp.mean(values, axis=-1, keepdims=True))
    variance = lax.optimization_barrier(jnp.mean(centred * centred, axis=-1, keepdims=True))
    return centred * lax.rsqrt(variance + epsilon) * gain_vector + bias_vector

def batch_moments(first_sum, second_sum, token_count):
    average = first_sum / token_count
    variance = second_sum / token_count - average * average
    return (average, lax.rsqrt(variance + epsilon))

def micro_forward(images_mb, probes_mb, subnet_code, params):
    expand_weight, batch_gain, batch_bias, depth_one, squeeze_weight, squeeze_bias, excite_weight, excite_bias, project_weight, norm_gain, norm_bias, qkv_weight, talk_before, talk_after, output_weight, output_bias, mlp_gain, mlp_bias, hidden_weight, hidden_bias, depth_two, return_weight, return_bias = params
    image_side, pixels, channel_mask, head_mask, unit_mask = code_masks(subnet_code)
    token_count = (IMGS * image_side * image_side).astype(jnp.float32)
    score_scale = HD ** (-0.5)
    masked = images_mb * pixels[None, :, None]
    expanded = low_back(jnp.einsum('npd,de->npe', masked, expand_weight, precision=highest))
    average, inverse = batch_moments(lax.optimization_barrier(jnp.sum(expanded, axis=(0, 1))), lax.optimization_barrier(jnp.sum(expanded * expanded, axis=(0, 1))), token_count)
    bundle = 8

    def shaped(array):
        return array.reshape((IMGS // bundle, bundle) + array.shape[1:])

    def bundle_forward(pieces):
        masked_b, expanded_b, probe_b = pieces
        normed = (expanded_b - average) * inverse * batch_gain + batch_bias
        activated = jax.nn.silu(normed) * channel_mask * pixels[:, None]
        deepened = depthwise(activated, depth_one) * pixels[:, None]
        pooled = lax.optimization_barrier(jnp.sum(deepened, axis=1)) / (image_side * image_side).astype(jnp.float32)
        squeezed = jax.nn.silu(jnp.dot(pooled, squeeze_weight, precision=highest) + squeeze_bias)
        excite = jax.nn.sigmoid(jnp.dot(squeezed, excite_weight, precision=highest) + excite_bias)
        scaled = low(deepened * excite[:, None, :])
        branch = low_back(jnp.einsum('npe,ed->npd', scaled, project_weight, precision=highest))
        handed = low(low_back(masked_b + branch)) + probe_b
        normed_one = low(layer_norm(handed, norm_gain, norm_bias))
        projected = low(low_back(jnp.einsum('npd,de->npe', normed_one, qkv_weight, precision=highest)))
        pieces_qkv = projected.reshape(bundle, PIX, 3, HEADS, HD)
        queries = pieces_qkv[:, :, 0]
        key_rows = pieces_qkv[:, :, 1]
        value_rows = pieces_qkv[:, :, 2] * head_mask[:, None]
        scores = low_back(jnp.einsum('nphc,nqhc->nhpq', queries, key_rows, precision=highest) * score_scale)
        mixture = jnp.einsum('hg,ngpq->nhpq', talk_before * head_mask, scores, precision=highest)
        mixture = jnp.where(pixels > 0.5, mixture, -1000000000.0)
        softmaxed = jax.nn.softmax(mixture, axis=-1)
        blended = low(jnp.einsum('hg,ngpq->nhpq', talk_after * head_mask, softmaxed, precision=highest))
        heads_out = jnp.einsum('nhpq,nqhc->nphc', blended, value_rows, precision=highest).reshape(bundle, PIX, D)
        heads_out = low(low_back(heads_out))
        attended = (low_back(jnp.einsum('npd,de->npe', heads_out, output_weight, precision=highest)) + output_bias) * pixels[:, None]
        middle = handed + attended
        normed_two = low(layer_norm(middle, mlp_gain, mlp_bias))
        hidden = (low_back(jnp.einsum('npd,df->npf', normed_two, hidden_weight, precision=highest)) + hidden_bias) * unit_mask * pixels[:, None]
        convolved = depthwise(hidden, depth_two) * pixels[:, None]
        activated_two = low(jax.nn.silu(convolved))
        output = low_back(jnp.einsum('npf,fd->npd', activated_two, return_weight, precision=highest)) + return_bias
        return ((middle + output) * pixels[:, None], handed)
    finals, handed_all = lax.map(jax.checkpoint(bundle_forward), (shaped(masked), shaped(expanded), shaped(probes_mb)))
    return (finals.reshape(images_mb.shape), handed_all.reshape(images_mb.shape))

def reference(images, codes, cotangent, expand_weight, batch_gain, batch_bias, depth_one, squeeze_weight, squeeze_bias, excite_weight, excite_bias, project_weight, norm_gain, norm_bias, qkv_weight, talk_before, talk_after, output_weight, output_bias, mlp_gain, mlp_bias, hidden_weight, hidden_bias, depth_two, return_weight, return_bias):
    params = tuple((member.astype(jnp.float32) for member in (expand_weight, batch_gain, batch_bias, depth_one, squeeze_weight, squeeze_bias, excite_weight, excite_bias, project_weight, norm_gain, norm_bias, qkv_weight, talk_before, talk_after, output_weight, output_bias, mlp_gain, mlp_bias, hidden_weight, hidden_bias, depth_two, return_weight, return_bias)))
    images_full = images.astype(jnp.float32)
    probes = jnp.zeros(images.shape, jnp.float32)

    def entire(images_in, probes_in, params_in):

        def micro_step(running, inputs):
            images_mb, probes_mb, subnet_code = inputs
            finals_mb, handed_mb = micro_forward(images_mb, probes_mb, subnet_code, params_in)
            return (running, (finals_mb, handed_mb))
        ignored, outcomes = lax.scan(jax.checkpoint(micro_step), jnp.zeros((), jnp.float32), (images_in, probes_in, codes))
        return (outcomes[0], outcomes[1])
    finals, pullback, handed_all = jax.vjp(entire, images_full, probes, params, has_aux=True)
    grad_images, grad_probes, gradients = pullback(cotangent.astype(jnp.float32))
    activations = jnp.stack([handed_all, finals]).astype(jnp.bfloat16)
    input_grads = jnp.stack([grad_images, grad_probes])
    return (activations, input_grads, *gradients)
```

```python
import functools
import math

import jax
import jax.numpy as jnp
from jax import lax
from jax.experimental import pallas as pl
from jax.experimental.pallas import tpu as pltpu
from jax.sharding import PartitionSpec as P

D = 216
E = 1296
SQ = 324
HEADS = 12
HD = 18
F = 864
SIDE = 14
PIX = 196
EPSILON = 1e-05
LOG2E = 1.4426950408889634

WIDE = 16
ROWS = SIDE * WIDE
LANES = 128
EB = -(-E // LANES)
FB = -(-F // LANES)
DB = -(-D // LANES)
EP = EB * LANES
FP = FB * LANES
DP = DB * LANES
QB = -(-3 * D // LANES)
QP = QB * LANES

PROJECT = 0
HIDDEN = PROJECT + EB
RETURN = HIDDEN + FB
QKV = RETURN + FB
OUTPUT = QKV + QB
COVARIANCE = OUTPUT + DB
EXPAND = COVARIANCE + DB
BLOCKS = EXPAND + EB - 1
TILES = ROWS // 16
ALL_TILES = BLOCKS * TILES
SHARED = QKV + QB - 1
HALF = LANES // 2
PARTS = 2
FACTOR_ROWS = 32
WEIGHTS = 18
UNPACKED = 26

f32 = jnp.float32
bf16 = jnp.bfloat16
HIGHEST = lax.Precision.HIGHEST
MIB = 1 << 20


def dot(a, b, contract=((1,), (0,)), precision=None):
    return lax.dot_general(a, b, (contract, ((), ())), preferred_element_type=f32, precision=precision)


NT = ((1,), (1,))


def iota(shape, dim):
    return lax.broadcasted_iota(jnp.int32, shape, dim)


def sigmoid(v):
    return 0.5 * jnp.tanh(0.5 * v) + 0.5


def grid_mask(shape, side):
    row = iota(shape, 0)
    return jnp.where(((row >> 4) < side) & ((row & 15) < side), 1.0, 0.0)


def widen(tokens, side):
    row = iota((ROWS, PIX), 0)
    hit = iota((ROWS, PIX), 1) == (row >> 4) * SIDE + (row & 15)
    pick = jnp.where(hit & ((row >> 4) < side) & ((row & 15) < side), 1.0, 0.0).astype(bf16)
    return dot(pick, tokens)


def narrow(tokens):
    column = iota((PIX, ROWS), 1)
    hit = iota((PIX, ROWS), 0) == (column >> 4) * SIDE + (column & 15)
    pick = jnp.where(hit & ((column & 15) < SIDE), 1.0, 0.0).astype(bf16)
    return dot(pick, tokens)


def narrow_into(ref, tokens):
    for i in range(SIDE):
        ref[i * SIDE : (i + 1) * SIDE, :] = tokens[i * WIDE : i * WIDE + SIDE, :]


def grid(v):
    return v.reshape(SIDE, WIDE, v.shape[-1])


def flat(v):
    return v.reshape(ROWS, v.shape[-1])


def depthwise(v, kernel):
    zero = jnp.zeros((1, WIDE, v.shape[-1]), f32)
    v3 = grid(v)
    above = flat(jnp.concatenate([zero, v3[:-1]], axis=0))
    below = flat(jnp.concatenate([v3[1:], zero], axis=0))
    left, middle, right = (kernel[b] * above + kernel[3 + b] * v + kernel[6 + b] * below for b in range(3))
    return middle + pltpu.roll(left, 1, 0) + pltpu.roll(right, ROWS - 1, 0)


def depthwise_kernel_grad(grad, v):
    g3 = grid(grad)
    shifted = [grid(pltpu.roll(v, 1, 0)), grid(v), grid(pltpu.roll(v, ROWS - 1, 0))]
    taps = []
    for a in (-1, 0, 1):
        for b in range(3):
            if a < 0:
                product = g3[1:] * shifted[b][:-1]
            elif a > 0:
                product = g3[:-1] * shifted[b][1:]
            else:
                product = g3 * shifted[b]
            taps.append(jnp.sum(jnp.sum(product, axis=0), axis=0, keepdims=True))
    return taps


def norm_forward(v):
    centred = v - jnp.sum(v, axis=-1, keepdims=True) * (1.0 / D)
    rs = lax.rsqrt(jnp.sum(centred * centred, axis=-1, keepdims=True) * (1.0 / D) + EPSILON)
    return centred * rs, rs


def norm_backward(grad, hat, rs, gain):
    scaled = grad * gain
    first = jnp.sum(scaled, axis=-1, keepdims=True) * (1.0 / D)
    second = jnp.sum(scaled * hat, axis=-1, keepdims=True) * (1.0 / D)
    return rs * (scaled - first - hat * second)


def row_sum(v):
    return jnp.sum(v, axis=0, keepdims=True)


def vector_times(row, matrix, contract):
    high = row.astype(bf16).astype(f32)
    rest = row - high
    mid = rest.astype(bf16).astype(f32)
    low = rest - mid
    which = iota((16, row.shape[-1]), 0)
    stack = jnp.where(which == 0, high, jnp.where(which == 1, mid, jnp.where(which == 2, low, 0.0)))
    return row_sum(dot(stack.astype(bf16), matrix, contract))


def moments(sums, count):
    average = sums[0:1] / count
    variance = sums[1:2] / count - average * average
    return average, lax.rsqrt(variance + EPSILON)


def put_block(tiles_ref, block, grad, smalls):
    tiles_ref[block * TILES : (block + 1) * TILES] = (
        jnp.concatenate([grad, smalls], axis=0).astype(bf16).reshape(TILES, 16, LANES)
    )


def block_of(v, b):
    return v[:, b * LANES : (b + 1) * LANES]


def code_of(codes):
    mine = lax.axis_index("pipe")
    return SIDE - 4 + 2 * codes[mine, 3], codes[mine, 0], codes[mine, 1], codes[mine, 2]


def home_of(order):
    spot = lax.axis_index("dp")
    home = lax.axis_index("pipe")
    for b in order:
        home = home * 2 + ((spot >> b) & 1)
    return home


def fetch(sources, targets, sems):
    copies = [pltpu.make_async_copy(a, b, sems.at[i]) for i, (a, b) in enumerate(zip(sources, targets))]
    for copy in copies:
        copy.start()
    return copies


def sums_kernel(codes, image, expand_hbm, sums_out, expand, sems):
    (expand_copy,) = fetch([expand_hbm], [expand], sems)
    side = code_of(codes)[0]
    tokens = widen(image[...], side).astype(bf16)
    expand_copy.wait()
    expanded = dot(tokens, expand[...])
    sums_out[0:1, :] = row_sum(expanded)
    sums_out[1:2, :] = row_sum(expanded * expanded)
    sums_out[2:3, :] = jnp.zeros((1, E), f32)
    sums_out[2:3, :D] = row_sum(tokens.astype(f32))


def middle_kernel(
    images_total,
    pieces,
    orders,
    codes,
    image,
    cotangent,
    sums,
    gain,
    bias,
    squeeze_bias,
    excite_bias,
    hidden_bias,
    *refs,
):
    (
        first_out,
        second_out,
        handed_grad_out,
        handed_low_out,
        tokens_out,
        expanded_grad_out,
        batch_out,
        kept_out,
        sent_out,
        factors_out,
        tiles_out,
        wide_e,
        wide_f,
        live,
        expanded_s,
        deep_s,
        scaled_s,
        soft_s,
        all_soft,
        all_grad,
        all_keys,
        all_values,
        hidden_s,
        conv_s,
        active_s,
        hidden_low_s,
        up_s,
        smalls_e,
        tail_e,
        smalls_f,
        grad_k,
        grad_v,
        talk_s,
        projected_s,
    ) = refs[WEIGHTS:]
    (
        expand,
        depth_one,
        squeeze_t,
        excite,
        project_t,
        norm_gain,
        norm_bias,
        qkv,
        talk_before,
        talk_after,
        output,
        output_bias,
        mlp_gain,
        mlp_bias,
        hidden,
        depth_two,
        return_t,
        return_bias,
    ) = refs[:WEIGHTS]
    side, code_channels, code_heads, code_units = code_of(codes)
    pixels = (side * side).astype(f32)
    count = images_total * pixels
    live[...] = grid_mask((ROWS, LANES), side)
    live_d = grid_mask((ROWS, D), side)

    average, inverse = moments(sums[...], count)
    wide_e[...] = jnp.zeros_like(wide_e)
    channel_mask = jnp.where(iota((1, E), 1) < E - (2 - code_channels) * D, 1.0, 0.0)
    wide_e[0:1, :E] = average
    wide_e[1:2, :E] = inverse * gain[...]
    wide_e[2:3, :E] = bias[...]
    wide_e[3:4, :E] = channel_mask
    wide_e[4:13, :E] = depth_one[...]
    wide_e[15:16, :E] = inverse
    tokens = widen(image[...], side).astype(bf16)
    tokens_out[...] = tokens
    token_mean = sums[2:3, :D] / count
    centred_tokens = (tokens.astype(f32) - token_mean) * live_d
    expanded_s[:, E - E % LANES :] = jnp.zeros((ROWS, EP - E + E % LANES), f32)
    expanded_s[:, :E] = dot(tokens, expand[...])

    def activate(at):
        centred = expanded_s[:, at] - wide_e[0:1, at]
        normed = centred * wide_e[1:2, at] + wide_e[2:3, at]
        gate = sigmoid(normed)
        return centred, normed, gate

    def forward_one(c, carry):
        at = pl.ds(pl.multiple_of(c * LANES, LANES), LANES)
        centred, normed, gate = activate(at)
        active = normed * gate * (live[...] * wide_e[3:4, at])
        deep = depthwise(active, [wide_e[4 + t : 5 + t, at] for t in range(9)]) * live[...]
        deep_s[:, at] = deep
        wide_e[14:15, at] = row_sum(deep) / pixels
        return carry

    lax.fori_loop(0, EB, forward_one, 0)
    pooled = wide_e[14:15, :E]
    squeeze_pre = vector_times(pooled, squeeze_t[...], NT) + squeeze_bias[...]
    squeeze_gate = sigmoid(squeeze_pre)
    squeezed = squeeze_pre * squeeze_gate
    excited = sigmoid(vector_times(squeezed, excite[...], ((1,), (0,))) + excite_bias[...])
    wide_e[13:14, :E] = excited
    scaled_s[...] = (deep_s[...] * wide_e[13:14, :]).astype(bf16)
    branch = dot(scaled_s[:, :E], project_t[...], NT)
    handed_low = (tokens.astype(f32) + branch).astype(bf16)
    first_out[...] = narrow(handed_low).astype(bf16)
    handed = handed_low.astype(f32)

    hat_one, rs_one = norm_forward(handed)
    normed_one = (hat_one * norm_gain[...] + norm_bias[...]).astype(bf16)
    projected = dot(normed_one, qkv[...]).astype(bf16).astype(f32)
    queries = projected[:, :D]
    key_rows_f = projected[:, D : 2 * D]
    live_heads = HEADS - 2 * (2 - code_heads)
    head_columns = iota((HEADS, D), 1)
    head_rows = iota((HEADS, D), 0) * HD
    own = jnp.where((head_columns >= head_rows) & (head_columns < head_rows + HD), 1.0, 0.0)
    own_rows = iota((D, HEADS), 0)
    own_columns = iota((D, HEADS), 1) * HD
    own_t = jnp.where((own_rows >= own_columns) & (own_rows < own_columns + HD), 1.0, 0.0)
    head_row = jnp.where(iota((1, HEADS), 1) < live_heads, 1.0, 0.0)
    head_column = jnp.where(iota((HEADS, 1), 0) < live_heads, 1.0, 0.0)
    value_mask = jnp.where(iota((1, D), 1) < live_heads * HD, 1.0, 0.0)
    before = talk_before[...] * head_row * HD ** (-0.5)
    after = talk_after[...] * head_row
    before_rows = dot(before, own, precision=HIGHEST)
    before_columns = dot(own_t, before, NT, precision=HIGHEST)
    after_rows = dot(after, own, ((0,), (0,)), precision=HIGHEST)
    after_columns = dot(own_t, after, precision=HIGHEST)
    value_rows_f = projected[:, 2 * D :] * value_mask
    queries_low = queries.astype(bf16)
    spare = iota((ROWS, DP), 1) == D
    row_place = iota((ROWS, DP), 0)
    dead = ((row_place >> 4) >= side) | ((row_place & 15) >= side)
    no_columns = jnp.zeros((ROWS, DP - D), f32)
    keys_wide = jnp.concatenate([key_rows_f, no_columns], axis=1)
    keys_wide = jnp.where(spare & dead, -1000000000.0, keys_wide)
    queries_wide = jnp.where(spare, 1.0, jnp.concatenate([queries, no_columns], axis=1))
    queries_t = queries_wide.T.astype(bf16)
    queries_twice = jnp.concatenate([queries_t, queries_t], axis=0)
    before_wide = jnp.concatenate([before_rows * LOG2E, jnp.zeros((HEADS, DP - D), f32)], axis=1)
    before_wide = jnp.where(iota((HEADS, DP), 1) == D, 1.0, before_wide)
    keys_t = key_rows_f.T
    values_t = value_rows_f.T
    all_soft[...] = jnp.zeros_like(all_soft)
    all_grad[...] = jnp.zeros_like(all_grad)
    all_keys[...] = jnp.zeros_like(all_keys)
    all_values[...] = jnp.zeros_like(all_values)
    for h in range(HEADS):
        weighted = keys_wide * before_wide[h : h + 1]
        high = weighted.astype(bf16)
        low = (weighted - high.astype(f32)).astype(bf16)
        scores = dot(jnp.concatenate([high, low], axis=1), queries_twice)
        grown = jnp.exp2(scores - jnp.max(scores, axis=0, keepdims=True))
        soft = grown * (1.0 / row_sum(grown))
        soft_s[h] = soft
        all_soft[h, 0:ROWS] = soft.astype(bf16)
        all_values[:, h * DP : h * DP + ROWS] = (values_t * after_columns[:, h : h + 1]).astype(bf16)
        all_keys[:, h * DP : h * DP + ROWS] = (keys_t * before_columns[:, h : h + 1]).astype(bf16)
    heads_out_t = dot(all_values[...], all_soft[...].reshape(HEADS * DP, ROWS)).astype(bf16)
    heads_out = heads_out_t.astype(f32).T.astype(bf16)
    attended = dot(heads_out, output[...]) + output_bias[...]
    middle = handed + attended * live_d

    hat_two, rs_two = norm_forward(middle)
    normed_two_f = hat_two * mlp_gain[...] + mlp_bias[...]
    normed_two = normed_two_f.astype(bf16)
    wide_f[...] = jnp.zeros_like(wide_f)
    wide_f[0:1, :F] = hidden_bias[...]
    wide_f[1:2, :F] = jnp.where(iota((1, F), 1) < F - (2 - code_units) * D, 1.0, 0.0)
    wide_f[2:11, :F] = depth_two[...]
    hidden_s[:, F - F % LANES :] = jnp.zeros((ROWS, FP - F + F % LANES), f32)
    hidden_s[:, :F] = dot(normed_two, hidden[...])

    def forward_two(c, carry):
        at = pl.ds(pl.multiple_of(c * LANES, LANES), LANES)
        units = (hidden_s[:, at] + wide_f[0:1, at]) * (live[...] * wide_f[1:2, at])
        hidden_s[:, at] = units
        conv = depthwise(units, [wide_f[2 + t : 3 + t, at] for t in range(9)]) * live[...]
        conv_s[:, at] = conv
        active_s[:, at] = (conv * sigmoid(conv)).astype(bf16)
        return carry

    lax.fori_loop(0, FB, forward_two, 0)
    final = middle + dot(active_s[:, :F], return_t[...], NT) + return_bias[...]
    second_out[...] = narrow((final * live_d).astype(bf16)).astype(bf16)

    upstream = widen(cotangent[...], side)
    grad_return_bias = row_sum(upstream)
    up_s[:, F - F % LANES :] = jnp.zeros((ROWS, FP - F + F % LANES), f32)
    up_s[:, :F] = dot(upstream.astype(bf16), return_t[...])
    smalls_f[...] = jnp.zeros_like(smalls_f)

    def backward_two(c, carry):
        at = pl.ds(pl.multiple_of(c * LANES, LANES), LANES)
        conv = conv_s[:, at]
        gate = sigmoid(conv)
        grad_conv = up_s[:, at] * (gate * (1.0 + conv * (1.0 - gate))) * live[...]
        taps = depthwise_kernel_grad(grad_conv, hidden_s[:, at])
        for t in range(9):
            smalls_f[t : t + 1, at] = taps[t]
        flipped = [wide_f[10 - t : 11 - t, at] for t in range(9)]
        grad_units = depthwise(grad_conv, flipped) * (live[...] * wide_f[1:2, at])
        smalls_f[9:10, at] = row_sum(grad_units)
        hidden_low_s[:, at] = grad_units.astype(bf16)
        return carry

    lax.fori_loop(0, FB, backward_two, 0)
    grad_return = dot(upstream.T.astype(bf16), active_s[...])
    for b in range(FB):
        put_block(tiles_out, RETURN + b, block_of(grad_return, b), smalls_f[8:16, b * LANES : (b + 1) * LANES])
    grad_hidden = dot(normed_two_f.T.astype(bf16), hidden_low_s[...])
    for b in range(FB):
        put_block(tiles_out, HIDDEN + b, block_of(grad_hidden, b), smalls_f[0:8, b * LANES : (b + 1) * LANES])
    grad_normed_two = dot(hidden_low_s[:, :F], hidden[...], NT)
    grad_mlp_gain = row_sum(grad_normed_two * hat_two)
    grad_mlp_bias = row_sum(grad_normed_two)
    grad_middle = upstream + norm_backward(grad_normed_two, hat_two, rs_two, mlp_gain[...])

    attend_up = grad_middle * live_d
    grad_output_bias = row_sum(attend_up)
    attend_low = attend_up.astype(bf16)
    grad_output = dot(heads_out_t, attend_low)
    grad_heads_low = dot(attend_low, output[...], NT).astype(bf16)
    grad_heads_t = grad_heads_low.astype(f32).T.astype(bf16)
    grad_k[...] = jnp.zeros_like(grad_k)
    grad_v[...] = jnp.zeros_like(grad_v)
    for h in range(HEADS):
        soft = soft_s[h]
        grad_soft = dot((value_rows_f * after_rows[h : h + 1]).astype(bf16), grad_heads_t)
        grad_scores = (soft * (grad_soft - row_sum(soft * grad_soft))).astype(bf16)
        all_grad[h, 0:ROWS] = grad_scores
        back = dot(grad_scores, queries_low)
        grad_k[...] += back * before_rows[h : h + 1]
        talk_s[h : h + 1, :] = row_sum(back * key_rows_f)
        back = dot(all_soft[h, 0:ROWS], grad_heads_low)
        grad_v[...] += back * after_rows[h : h + 1]
        talk_s[16 + h : 17 + h, :] = row_sum(back * value_rows_f)
    grad_q = dot(all_keys[...], all_grad[...].reshape(HEADS * DP, ROWS)).T
    talk_before_grad = dot(talk_s[0:12, :], own_t, precision=HIGHEST) * (head_row * HD ** (-0.5))
    talk_after_grad = dot(own_t, talk_s[16:28, :], ((0,), (1,)), precision=HIGHEST) * head_row
    projected_s[:, :D] = grad_q
    projected_s[:, D : 2 * D] = grad_k[...]
    projected_s[:, 2 * D :] = grad_v[...] * value_mask
    grad_projected = projected_s[...].astype(bf16)
    grad_normed_one = dot(grad_projected, qkv[...], NT)
    normed_one_t = (hat_one * norm_gain[...] + norm_bias[...]).T.astype(bf16)
    grad_norm_gain = row_sum(grad_normed_one * hat_one)
    grad_norm_bias = row_sum(grad_normed_one)
    handed_grad = grad_middle + norm_backward(grad_normed_one, hat_one, rs_one, norm_gain[...])
    narrow_into(handed_grad_out, handed_grad)

    talk_s[...] = jnp.zeros_like(talk_s)
    talk_s[0:12, 0:HEADS] = talk_before_grad
    talk_s[16:28, 0:HEADS] = talk_after_grad
    grad_qkv = jnp.concatenate([dot(normed_one_t, grad_projected), jnp.zeros((D, QP - 3 * D), f32)], axis=1)
    for b in range(QB - 1):
        extra = talk_s[8 * b : 8 * b + 8, 0:LANES] if b < 4 else jnp.zeros((8, LANES), f32)
        put_block(tiles_out, QKV + b, block_of(grad_qkv, b), extra)
    talk_s[0:8, :] = jnp.zeros((8, D), f32)
    talk_s[0:1, :] = grad_norm_gain
    talk_s[1:2, :] = grad_norm_bias
    talk_s[2:3, :] = grad_output_bias
    talk_s[3:4, :] = grad_mlp_gain
    talk_s[4:5, :] = grad_mlp_bias
    talk_s[5:6, :] = grad_return_bias
    leading = lax.axis_index("pipe") == 0
    centred_low = centred_tokens.astype(bf16)
    centred_t = centred_tokens.T.astype(bf16)
    covariance = dot(centred_t, centred_low)
    over = iota((D, D), 0) - iota((D, D), 1)
    over = jnp.where(leading, over, -over)
    talk_s[6:7, :] = jnp.where(leading, 0.0, row_sum(jnp.where(over == 0, covariance, 0.0)))
    wanted = (over < 0) | ((over == 0) & leading)
    covariance = jnp.concatenate([jnp.where(wanted, covariance, 0.0), jnp.zeros((D, DP - D), f32)], axis=1)
    for b in range(DB):
        put_block(tiles_out, COVARIANCE + b, block_of(covariance, b), jnp.zeros((8, LANES), f32))
    for b in range(DB):
        piece = jnp.concatenate([grad_output, jnp.zeros((D, DP - D), f32)], axis=1)
        extra = jnp.concatenate([talk_s[0:8, :], jnp.zeros((8, DP - D), f32)], axis=1)
        put_block(tiles_out, OUTPUT + b, block_of(piece, b), block_of(extra, b))

    back_low = handed_grad.astype(bf16)
    handed_low_out[...] = back_low
    expanded_grad_out[:, E - E % LANES :] = jnp.zeros((ROWS, EP - E + E % LANES), f32)
    expanded_grad_out[:, :E] = dot(back_low, project_t[...])

    excited = wide_e[13:14, :E]
    grad_excited = row_sum(expanded_grad_out[:, :E] * deep_s[:, :E])
    grad_excite_pre = grad_excited * excited * (1.0 - excited)
    grad_squeezed = vector_times(grad_excite_pre, excite[...], NT)
    grad_squeeze_pre = grad_squeezed * (squeeze_gate * (1.0 + squeeze_pre * (1.0 - squeeze_gate)))
    grad_pooled = vector_times(grad_squeeze_pre, squeeze_t[...], ((1,), (0,)))
    factors_out[...] = jnp.zeros_like(factors_out)

    def put_factor(start, row):
        width = row.shape[-1]
        for b in range(-(-width // LANES)):
            end = min(width, (b + 1) * LANES)
            factors_out[start + b : start + b + 1, 0 : end - b * LANES] = row[:, b * LANES : end]

    put_factor(0, wide_e[14:15, :E])
    put_factor(EB, grad_excite_pre)
    put_factor(2 * EB, squeezed)
    put_factor(2 * EB + 3, grad_squeeze_pre)
    wide_e[14:15, :E] = grad_pooled / pixels
    tail_e[...] = jnp.zeros_like(tail_e)
    batch_out[...] = jnp.zeros_like(batch_out)

    def backward_one(c, carry):
        at = pl.ds(pl.multiple_of(c * LANES, LANES), LANES)
        centred, normed, gate = activate(at)
        mask = live[...] * wide_e[3:4, at]
        active = normed * gate * mask
        grad_deep = (expanded_grad_out[:, at] * wide_e[13:14, at] + wide_e[14:15, at]) * live[...]
        taps = depthwise_kernel_grad(grad_deep, active)
        for t in range(8):
            smalls_e[t : t + 1, at] = taps[t]
        flipped = [wide_e[12 - t : 13 - t, at] for t in range(9)]
        grad_active = depthwise(grad_deep, flipped) * mask
        grad_normed = grad_active * (gate * (1.0 + normed * (1.0 - gate)))
        grad_gain = row_sum(grad_normed * centred) * wide_e[15:16, at]
        grad_bias = row_sum(grad_normed)
        batch_out[pl.ds(c, 1), :] = grad_gain
        batch_out[pl.ds(c + 16, 1), :] = grad_bias
        tail_e[0:1, at] = grad_gain
        tail_e[1:2, at] = grad_bias
        tail_e[2:3, at] = taps[8]
        grad_second = grad_gain * wide_e[15:16, at] * wide_e[1:2, at] * (-1.0 / count)
        tail_e[3:4, at] = jnp.where(leading, grad_second, 0.0)
        tail_e[4:5, at] = jnp.where(leading, 0.0, grad_second)
        expanded_grad_out[:, at] = grad_normed * wide_e[1:2, at]
        return carry

    lax.fori_loop(0, EB, backward_one, 0)
    grad_project = dot(handed_grad.T.astype(bf16), scaled_s[...])
    for b in range(EB):
        put_block(tiles_out, PROJECT + b, block_of(grad_project, b), smalls_e[:, b * LANES : (b + 1) * LANES])
    grad_expand = dot(centred_t, expanded_grad_out[...].astype(bf16))
    for b in range(EB - 1):
        put_block(tiles_out, EXPAND + b, block_of(grad_expand, b), tail_e[:, b * LANES : (b + 1) * LANES])
    last = jnp.concatenate([block_of(grad_expand, EB - 1), tail_e[:, EP - LANES :]], axis=0)
    shared = jnp.concatenate([block_of(grad_qkv, QB - 1), jnp.zeros((8, LANES), f32)], axis=0)
    shared = shared + pltpu.roll(last, HALF, 1)
    put_block(tiles_out, SHARED, shared[:D], shared[D:])
    spare = tiles_out.shape[0] - ALL_TILES
    if spare:
        tiles_out[ALL_TILES:] = jnp.zeros((spare, 16, LANES), bf16)

    half = pieces // 2
    per_piece = kept_out.shape[2]
    for part, order in enumerate(orders):
        me = home_of(order) & (half - 1)
        for piece in range(half):
            first = (part * pieces + piece) * per_piece
            second = first + half * per_piece
            low = tiles_out[first : first + per_piece]
            high = tiles_out[second : second + per_piece]
            kept_out[piece ^ me, part] = jnp.where(leading, low, high)
            sent_out[piece ^ me, part] = jnp.where(leading, high, low)


def last_kernel(
    images_total, codes, sums, total, gain, tokens, handed_low, expanded_grad, expand, grad_out, wide
):
    side = code_of(codes)[0]
    count = images_total * (side * side).astype(f32)
    average, inverse = moments(sums[...], count)
    scale = inverse * gain[...]
    for b in range(EB):
        wide[0:1, b * LANES : (b + 1) * LANES] = total[b : b + 1, :]
        wide[1:2, b * LANES : (b + 1) * LANES] = total[16 + b : 17 + b, :]
    grad_variance = -0.5 * inverse * scale * wide[0:1, :E]
    grad_second = grad_variance / count
    grad_first = (-scale * wide[1:2, :E] - 2.0 * average * grad_variance) / count
    expanded = dot(tokens[...], expand[...])
    grad = (expanded_grad[:, :E] + grad_first + 2.0 * expanded * grad_second).astype(bf16)
    grad_tokens = (handed_low[...].astype(f32) + dot(grad, expand[...], NT)) * grid_mask((ROWS, D), side)
    narrow_into(grad_out, grad_tokens)


def unpack_kernel(pieces, per_piece, orders, merged, *refs):
    expand, *refs = refs
    single = (len(refs) - UNPACKED - merged) // PARTS
    inputs = refs[: merged + PARTS * single]
    (
        expand_out,
        gain_out,
        bias_out,
        depth_one_out,
        squeeze_out,
        squeeze_bias_out,
        excite_out,
        excite_bias_out,
        project_out,
        norm_gain_out,
        norm_bias_out,
        qkv_out,
        talk_before_out,
        talk_after_out,
        output_out,
        output_bias_out,
        mlp_gain_out,
        mlp_bias_out,
        hidden_out,
        hidden_bias_out,
        depth_two_out,
        return_out,
        return_bias_out,
        tiles,
        factors,
        wide,
    ) = refs[merged + PARTS * single :]
    for part, order in enumerate(orders):
        me = home_of(order)
        at = 0
        own = inputs[merged + part * single : merged + (part + 1) * single]
        for number, ref in enumerate(inputs[:merged] + own):
            skipped = part * (per_piece + FACTOR_ROWS // 16) if number < merged else 0
            for inner in range(ref.shape[0]):
                home = at ^ me
                tiles[pl.ds((part * pieces + home) * per_piece, per_piece)] = ref[inner, skipped : skipped + per_piece]
                if part == 0:
                    factor = ref[inner, per_piece : per_piece + FACTOR_ROWS // 16]
                    factors[home] = factor.reshape(FACTOR_ROWS, LANES).astype(f32)
                at += 1

    def block(b):
        return tiles[b * TILES : (b + 1) * TILES].reshape(ROWS, LANES).astype(f32)

    def spread(first, count, width, out, take):
        for b in range(count):
            value = block(first + b)
            start, stop = b * LANES, min(width, (b + 1) * LANES)
            out[:, start:stop] = value[0:D, 0 : stop - start]
            for ref, top, row, rows in take:
                if len(ref.shape) == 1:
                    ref[start:stop] = value[D + row, 0 : stop - start]
                else:
                    ref[top : top + rows, start:stop] = value[D + row : D + row + rows, 0 : stop - start]

    spread(PROJECT, EB, E, project_out, [(depth_one_out, 0, 0, 8)])
    shared = pltpu.roll(block(SHARED), HALF, 1)
    for b in range(EB):
        value = block(EXPAND + b) if b < EB - 1 else shared
        wide[:, b * LANES : (b + 1) * LANES] = value
    gain_out[...] = wide[D, 0:E]
    bias_out[...] = wide[D + 1, 0:E]
    depth_one_out[8:9, :] = wide[D + 2 : D + 3, 0:E]
    both = jnp.concatenate([block(COVARIANCE), block(COVARIANCE + 1)], axis=1)[0:D, 0:D]
    turned = both.T
    over = iota((D, D), 0) - iota((D, D), 1)
    diagonal = jnp.concatenate([block(OUTPUT)[D + 6 : D + 7], block(OUTPUT + 1)[D + 6 : D + 7]], axis=1)[:, 0:D]
    first = jnp.where(over <= 0, both, turned).astype(bf16)
    second = jnp.where(over > 0, both, jnp.where(over < 0, turned, diagonal)).astype(bf16)
    added = dot(first, expand[...]) * wide[D + 3 : D + 4, 0:E] + dot(second, expand[...]) * wide[D + 4 : D + 5, 0:E]
    expand_out[...] = wide[0:D, 0:E] + added
    spread(HIDDEN, FB, F, hidden_out, [(depth_two_out, 0, 0, 8)])
    spread(RETURN, FB, F, return_out, [(depth_two_out, 8, 0, 1), (hidden_bias_out, 0, 1, 1)])
    vectors = (norm_gain_out, norm_bias_out, output_bias_out, mlp_gain_out, mlp_bias_out, return_bias_out)
    spread(OUTPUT, DB, D, output_out, [(ref, 0, row, 1) for row, ref in enumerate(vectors)])
    spread(QKV, QB, 3 * D, qkv_out, [])
    talk_before_out[0:8] = block(QKV)[D : D + 8, 0:HEADS]
    talk_before_out[8:12] = block(QKV + 1)[D : D + 4, 0:HEADS]
    talk_after_out[0:8] = block(QKV + 2)[D : D + 8, 0:HEADS]
    talk_after_out[8:12] = block(QKV + 3)[D : D + 4, 0:HEADS]

    def gathered(start, width):
        columns = [factors[:, start + b, :] for b in range(-(-width // LANES))]
        return jnp.concatenate(columns, axis=1)[:, 0:width]

    pooled = gathered(0, E)
    grad_excite_pre = gathered(EB, E)
    squeezed = gathered(2 * EB, SQ)
    grad_squeeze_pre = gathered(2 * EB + 3, SQ)
    squeeze_bias_out[...] = jnp.sum(grad_squeeze_pre, axis=0)
    excite_bias_out[...] = jnp.sum(grad_excite_pre, axis=0)
    squeeze_out[...] = dot(grad_squeeze_pre.T.astype(bf16), pooled.astype(bf16))
    excite_out[...] = dot(squeezed.T.astype(bf16), grad_excite_pre.astype(bf16))


def kernel_call(body, name, shapes, scratch, operands, fetched, limit, flops):
    in_specs = [pl.BlockSpec(memory_space=pltpu.VMEM)] * len(operands)
    if fetched is not None:
        in_specs[0] = pl.BlockSpec(memory_space=pltpu.SMEM)
        in_specs += [pl.BlockSpec(memory_space=pltpu.HBM)] * len(fetched)
    return pl.pallas_call(
        body,
        out_shape=[jax.ShapeDtypeStruct(shape, kind) for shape, kind in shapes],
        in_specs=in_specs,
        out_specs=[pl.BlockSpec(memory_space=pltpu.VMEM)] * len(shapes),
        scratch_shapes=scratch,
        compiler_params=pltpu.CompilerParams(vmem_limit_bytes=limit * MIB),
        cost_estimate=pl.CostEstimate(flops=flops, bytes_accessed=8 * MIB, transcendentals=0),
        name=name,
    )(*operands, *(fetched or ()))


def swapped(value, axis, mask):
    size = lax.axis_size(axis)
    return lax.ppermute(value, axis, [(i, i ^ mask) for i in range(size)])


def summed_over_dp(value, bits):
    for first in range(0, bits, 2):
        here = [1 << b for b in range(first, min(first + 2, bits))]
        masks = here + ([here[0] | here[1]] if len(here) == 2 else [])
        others = [swapped(value, "dp", mask) for mask in masks]
        value = value + functools.reduce(jnp.add, others)
    return value


def on_device(
    images,
    codes,
    cotangent,
    expand_weight,
    batch_gain,
    batch_bias,
    depth_one,
    squeeze_weight,
    squeeze_bias,
    excite_weight,
    excite_bias,
    project_weight,
    norm_gain,
    norm_bias,
    qkv_weight,
    talk_before,
    talk_after,
    output_weight,
    output_bias,
    mlp_gain,
    mlp_bias,
    hidden_weight,
    hidden_bias,
    depth_two,
    return_weight,
    return_bias,
):
    devices_dp = lax.axis_size("dp")
    bits = devices_dp.bit_length() - 1
    pieces = 2 * devices_dp
    half = pieces // 2
    images_total = float(images.shape[1] * devices_dp)
    per_piece = -(-ALL_TILES // (PARTS * pieces))
    factor_tiles = FACTOR_ROWS // 16
    pipe = lax.axis_index("pipe")

    rest = list(range(2, bits))
    groups = [rest[g : g + 2] for g in range(0, len(rest), 2)]
    orders = [[0, 1] + rest, [1, 0] + rest]
    image = lax.dynamic_index_in_dim(images, pipe, 0, keepdims=False)[0]
    upstream = lax.dynamic_index_in_dim(cotangent, pipe, 0, keepdims=False)[0]

    def row(vector):
        return vector.reshape(1, -1)

    def buffers(arrays):
        return [pltpu.VMEM(a.shape, a.dtype) for a in arrays]

    squeeze_t = squeeze_weight.T
    project_t = project_weight.T
    return_t = return_weight.T
    gain = row(batch_gain)

    (sums,) = kernel_call(
        sums_kernel,
        "sums",
        [((3, E), f32)],
        buffers([expand_weight]) + [pltpu.SemaphoreType.DMA((1,))],
        (codes, image),
        (expand_weight,),
        16,
        1 << 33,
    )
    sums = summed_over_dp(sums, bits)

    operands = (
        codes,
        image,
        upstream,
        sums,
        gain,
        row(batch_bias),
        row(squeeze_bias),
        row(excite_bias),
        row(hidden_bias),
        expand_weight,
        depth_one,
        squeeze_t,
        excite_weight,
        project_t,
        row(norm_gain),
        row(norm_bias),
        qkv_weight,
        talk_before,
        talk_after,
        output_weight,
        row(output_bias),
        row(mlp_gain),
        row(mlp_bias),
        hidden_weight,
        depth_two,
        return_t,
        row(return_bias),
    )
    shapes = [
        ((PIX, D), bf16),
        ((PIX, D), bf16),
        ((PIX, D), f32),
        ((ROWS, D), bf16),
        ((ROWS, D), bf16),
        ((ROWS, EP), f32),
        ((32, LANES), f32),
        ((half, PARTS, per_piece, 16, LANES), bf16),
        ((half, PARTS, per_piece, 16, LANES), bf16),
        ((FACTOR_ROWS, LANES), f32),
    ]
    scratch = [
        pltpu.VMEM((PARTS * pieces * per_piece, 16, LANES), bf16),
        pltpu.VMEM((16, EP), f32),
        pltpu.VMEM((16, FP), f32),
        pltpu.VMEM((ROWS, LANES), f32),
        pltpu.VMEM((ROWS, EP), f32),
        pltpu.VMEM((ROWS, EP), f32),
        pltpu.VMEM((ROWS, EP), bf16),
        pltpu.VMEM((HEADS, ROWS, ROWS), f32),
        pltpu.VMEM((HEADS, DP, ROWS), bf16),
        pltpu.VMEM((HEADS, DP, ROWS), bf16),
        pltpu.VMEM((D, HEADS * DP), bf16),
        pltpu.VMEM((D, HEADS * DP), bf16),
        pltpu.VMEM((ROWS, FP), f32),
        pltpu.VMEM((ROWS, FP), f32),
        pltpu.VMEM((ROWS, FP), bf16),
        pltpu.VMEM((ROWS, FP), bf16),
        pltpu.VMEM((ROWS, FP), f32),
        pltpu.VMEM((8, EP), f32),
        pltpu.VMEM((8, EP), f32),
        pltpu.VMEM((16, FP), f32),
        pltpu.VMEM((ROWS, D), f32),
        pltpu.VMEM((ROWS, D), f32),
        pltpu.VMEM((32, D), f32),
        pltpu.VMEM((ROWS, 3 * D), f32),
    ]
    first, second, handed_grad, handed_low, tokens, expanded_grad, batch, kept, sent, factors = kernel_call(
        functools.partial(middle_kernel, images_total, pieces, orders),
        "middle",
        shapes,
        scratch,
        operands,
        (),
        40,
        1 << 32,
    )

    def plus(value, *others):
        return functools.reduce(jnp.add, [v.astype(f32) for v in (value, *others)]).astype(bf16)

    def masks_of(group):
        return [sum(1 << b for i, b in enumerate(group) if (j >> (len(group) - 1 - i)) & 1) for j in range(1 << len(group))]

    def as_tiles(value):
        high = lax.reduce_precision(value, exponent_bits=8, mantissa_bits=7)
        return jnp.concatenate([high, value - high]).astype(bf16).reshape(-1, 16, LANES)

    def with_batch(value):
        return jnp.concatenate([value.reshape(-1, 16, LANES), as_tiles(batch)])

    def from_batch(value, like):
        count = math.prod(like.shape[:-2])
        rest_of = value[count:].astype(f32).reshape(2, -1, LANES)
        return value[:count].reshape(like.shape), rest_of[0] + rest_of[1]

    held = plus(kept, swapped(sent, "pipe", 1))
    held = [held[:, part] for part in range(PARTS)]
    for step in range(2):
        sending = [value[value.shape[0] // 2 :] for value in held]
        arrived = [swapped(with_batch(sending[0]), "dp", 1 << orders[0][step])]
        arrived += [swapped(value, "dp", 1 << order[step]) for value, order in zip(sending[1:], orders[1:])]
        arrived[0], other_batch = from_batch(arrived[0], sending[0])
        batch = batch + other_batch
        held = [plus(value[: value.shape[0] // 2], other) for value, other in zip(held, arrived)]
    held = jnp.concatenate(held, axis=1)
    for group in groups:
        masks = masks_of(group)
        quarters = held.reshape((len(masks), -1) + held.shape[1:])
        arrived = [swapped(with_batch(quarters[j]), "dp", masks[j]) for j in range(1, len(masks))]
        arrived = [from_batch(value, quarters[0]) for value in arrived]
        batch = batch + functools.reduce(jnp.add, [other for _, other in arrived])
        held = plus(quarters[0], *[value for value, _ in arrived])
    (images_grad,) = kernel_call(
        functools.partial(last_kernel, images_total),
        "last",
        [((PIX, D), f32)],
        [pltpu.VMEM((2, EP), f32)],
        (codes, sums, batch, gain, tokens, handed_low, expanded_grad, expand_weight),
        (),
        16,
        1 << 31,
    )

    held = jnp.concatenate(
        [held[:, :per_piece], factors.astype(bf16).reshape(1, factor_tiles, 16, LANES), held[:, per_piece:]], axis=1
    )
    merged = [held]
    for group in reversed(groups):
        merged += [swapped(held, "dp", mask) for mask in masks_of(group)[1:]]
        held = jnp.concatenate(merged, axis=0)
    widths = per_piece + factor_tiles
    held = [held[:, :widths], held[:, widths:]]
    collected = [[], []]
    for step in (1, 0):
        arrived = [swapped(value, "dp", 1 << order[step]) for value, order in zip(held, orders)]
        for part in range(PARTS):
            collected[part].append(arrived[part])
        held = [jnp.concatenate([value, other], axis=0) for value, other in zip(held, arrived)]
    for part in range(PARTS):
        collected[part].append(swapped(held[part], "pipe", 1))
    grads = kernel_call(
        functools.partial(unpack_kernel, pieces, per_piece, orders, len(merged)),
        "unpack",
        [
            ((D, E), f32),
            ((E,), f32),
            ((E,), f32),
            ((9, E), f32),
            ((SQ, E), f32),
            ((SQ,), f32),
            ((SQ, E), f32),
            ((E,), f32),
            ((D, E), f32),
            ((D,), f32),
            ((D,), f32),
            ((D, 3 * D), f32),
            ((HEADS, HEADS), f32),
            ((HEADS, HEADS), f32),
            ((D, D), f32),
            ((D,), f32),
            ((D,), f32),
            ((D,), f32),
            ((D, F), f32),
            ((F,), f32),
            ((9, F), f32),
            ((D, F), f32),
            ((D,), f32),
        ],
        [
            pltpu.VMEM((PARTS * pieces * per_piece, 16, LANES), bf16),
            pltpu.VMEM((pieces, FACTOR_ROWS, LANES), f32),
            pltpu.VMEM((ROWS, EP), f32),
        ],
        (expand_weight, *merged, *collected[0], *collected[1]),
        None,
        40,
        1 << 26,
    )
    grads = list(grads)
    for transposed in (4, 8, 21):
        grads[transposed] = grads[transposed].T

    leading = pipe == 0

    def both_layers(one, two):
        other = swapped(jnp.where(leading, two, one), "pipe", 1)
        return jnp.where(leading, jnp.stack([one, other]), jnp.stack([other, two]))[None, :, None]

    activations = both_layers(first, second)
    input_grads = both_layers(images_grad, handed_grad)
    return (activations, input_grads, *grads)


def solution(mesh):
    in_specs = (P(None, "dp", None, None), P(), P(None, "dp", None, None)) + (P(),) * 23
    out_specs = (P("pipe", None, "dp", None, None), P("pipe", None, "dp", None, None)) + (P(),) * 23
    return jax.shard_map(on_device, mesh=mesh, in_specs=in_specs, out_specs=out_specs, check_vma=False)
```

```python
import functools
import math

import jax
import jax.numpy as jnp
from jax import lax
from jax.experimental import pallas as pl
from jax.experimental.pallas import tpu as pltpu
from jax.sharding import PartitionSpec as P

D = 216
E = 1296
SQ = 324
HEADS = 12
HD = 18
F = 864
SIDE = 14
PIX = 196
EPSILON = 1e-05
LOG2E = 1.4426950408889634

WIDE = 16
ROWS = SIDE * WIDE
LANES = 128
EB = -(-E // LANES)
FB = -(-F // LANES)
DB = -(-D // LANES)
EP = EB * LANES
FP = FB * LANES
DP = DB * LANES
QB = -(-3 * D // LANES)
QP = QB * LANES

PROJECT = 0
HIDDEN = PROJECT + EB - 1
RETURN = HIDDEN + FB
QKV = RETURN + FB
OUTPUT = QKV + QB - 1
COVARIANCE = OUTPUT + DB
EXPAND = COVARIANCE + DB
BLOCKS = EXPAND + EB - 1
PROJECT_TAIL = HIDDEN + FB - 1
EXPAND_TAIL = RETURN + FB - 1
QKV_TAIL = OUTPUT + DB - 1
TAIL_LANE = 96
TILES = ROWS // 16
ALL_TILES = BLOCKS * TILES
PARTS = 2
RIDDEN = 1
FACTOR_ROWS = 32
WEIGHTS = 18
UNPACKED = 26

f32 = jnp.float32
bf16 = jnp.bfloat16
HIGHEST = lax.Precision.HIGHEST
MIB = 1 << 20


def dot(a, b, contract=((1,), (0,)), precision=None):
    return lax.dot_general(a, b, (contract, ((), ())), preferred_element_type=f32, precision=precision)


NT = ((1,), (1,))


def iota(shape, dim):
    return lax.broadcasted_iota(jnp.int32, shape, dim)


def sigmoid(v):
    return 0.5 * jnp.tanh(0.5 * v) + 0.5


def silu_and_slope(half, live):
    turn = jnp.tanh(half)
    more = 1.0 + turn
    return half * more, (more * (1.0 + half * (1.0 - turn))) * live


def grid_mask(shape, side):
    row = iota(shape, 0)
    return jnp.where(((row >> 4) < side) & ((row & 15) < side), 1.0, 0.0)


def widen(tokens, side):
    row = iota((ROWS, PIX), 0)
    hit = iota((ROWS, PIX), 1) == (row >> 4) * SIDE + (row & 15)
    pick = jnp.where(hit & ((row >> 4) < side) & ((row & 15) < side), 1.0, 0.0).astype(bf16)
    return dot(pick, tokens)


def narrow(tokens):
    column = iota((PIX, ROWS), 1)
    hit = iota((PIX, ROWS), 0) == (column >> 4) * SIDE + (column & 15)
    pick = jnp.where(hit & ((column & 15) < SIDE), 1.0, 0.0).astype(bf16)
    return dot(pick, tokens)


def narrow_into(ref, tokens):
    for i in range(SIDE):
        ref[i * SIDE : (i + 1) * SIDE, :] = tokens[i * WIDE : i * WIDE + SIDE, :]


def grid(v):
    return v.reshape(SIDE, WIDE, v.shape[-1])


def flat(v):
    return v.reshape(ROWS, v.shape[-1])


def sideways(ref, v):
    ref[8 : 8 + ROWS] = v
    return [ref[7 : 7 + ROWS], v, ref[9 : 9 + ROWS]]


def depthwise(three, kernel):
    rows = [sum(kernel[3 * a + b] * three[b] for b in range(3)) for a in range(3)]
    zero = jnp.zeros((1, WIDE, LANES), f32)
    above = flat(jnp.concatenate([zero, grid(rows[0])[:-1]], axis=0))
    below = flat(jnp.concatenate([grid(rows[2])[1:], zero], axis=0))
    return rows[1] + above + below


def depthwise_kernel_grad(three, v):
    v3 = grid(v)
    taps = []
    for a in (-1, 0, 1):
        for b in (-1, 0, 1):
            g3 = grid(three[1 - b])
            if a < 0:
                product = v3[:-1] * g3[1:]
            elif a > 0:
                product = v3[1:] * g3[:-1]
            else:
                product = v3 * g3
            taps.append(jnp.sum(jnp.sum(product, axis=0), axis=0, keepdims=True))
    return taps


def norm_forward(v):
    centred = v - jnp.sum(v, axis=-1, keepdims=True) * (1.0 / D)
    rs = lax.rsqrt(jnp.sum(centred * centred, axis=-1, keepdims=True) * (1.0 / D) + EPSILON)
    return centred * rs, rs


def norm_backward(grad, hat, rs, gain):
    scaled = grad * gain
    first = jnp.sum(scaled, axis=-1, keepdims=True) * (1.0 / D)
    second = jnp.sum(scaled * hat, axis=-1, keepdims=True) * (1.0 / D)
    return rs * (scaled - first - hat * second)


def row_sum(v):
    return jnp.sum(v, axis=0, keepdims=True)


def vector_times(row, matrix, contract):
    high = row.astype(bf16).astype(f32)
    rest = row - high
    mid = rest.astype(bf16).astype(f32)
    low = rest - mid
    which = iota((16, row.shape[-1]), 0)
    stack = jnp.where(which == 0, high, jnp.where(which == 1, mid, jnp.where(which == 2, low, 0.0)))
    return row_sum(dot(stack.astype(bf16), matrix, contract))


def moments(sums, count):
    average = sums[0:1] / count
    variance = sums[1:2] / count - average * average
    return average, lax.rsqrt(variance + EPSILON)


def put_block(tiles_ref, block, grad, smalls):
    tiles_ref[block * TILES : (block + 1) * TILES] = (
        jnp.concatenate([grad, smalls], axis=0).astype(bf16).reshape(TILES, 16, LANES)
    )


def add_tail(tiles_ref, block, grad, smalls):
    at = slice(block * TILES, (block + 1) * TILES)
    tail = pltpu.roll(jnp.concatenate([grad, smalls], axis=0), TAIL_LANE, 1)
    held = tiles_ref[at].reshape(ROWS, LANES).astype(f32)
    tiles_ref[at] = (held + tail).astype(bf16).reshape(TILES, 16, LANES)


def block_of(v, b):
    return v[:, b * LANES : (b + 1) * LANES]


def code_of(codes):
    mine = lax.axis_index("pipe")
    return SIDE - 4 + 2 * codes[mine, 3], codes[mine, 0], codes[mine, 1], codes[mine, 2]


def home_of(order):
    spot = lax.axis_index("dp")
    home = lax.axis_index("pipe")
    for b in order:
        home = home * 2 + ((spot >> b) & 1)
    return home


def fetch(sources, targets, sems):
    copies = [pltpu.make_async_copy(a, b, sems.at[i]) for i, (a, b) in enumerate(zip(sources, targets))]
    for copy in copies:
        copy.start()
    return copies


def sums_kernel(codes, image, expand_hbm, sums_out, expand, sems):
    (expand_copy,) = fetch([expand_hbm], [expand], sems)
    side = code_of(codes)[0]
    tokens = widen(image[...], side).astype(bf16)
    expand_copy.wait()
    expanded = dot(tokens, expand[...])
    sums_out[0:1, :] = row_sum(expanded)
    sums_out[1:2, :] = row_sum(expanded * expanded)
    sums_out[2:3, :] = jnp.zeros((1, E), f32)
    sums_out[2:3, :D] = row_sum(tokens.astype(f32))


def middle_kernel(
    images_total,
    pieces,
    per_piece,
    orders,
    codes,
    image,
    cotangent,
    sums,
    gain,
    bias,
    squeeze_bias,
    excite_bias,
    hidden_bias,
    *refs,
):
    (
        first_out,
        second_out,
        handed_grad_out,
        handed_low_out,
        tokens_out,
        expanded_grad_out,
        batch_out,
        kept_out,
        sent_out,
        factors_out,
        tiles_out,
        wide_e,
        wide_f,
        live,
        half_live,
        beside,
        half_scale,
        expanded_s,
        deep_grad,
        active_e,
        slope_e,
        deep_s,
        scaled_s,
        mixes,
        three_s,
        keys_wide,
        soft_s,
        all_soft,
        all_grad,
        all_keys,
        all_values,
        hidden_s,
        slope_s,
        active_s,
        hidden_low_s,
        up_s,
        smalls_e,
        tail_e,
        smalls_f,
        grad_k,
        grad_v,
        talk_s,
        projected_s,
    ) = refs[WEIGHTS:]
    (
        expand,
        depth_one,
        squeeze_t,
        excite,
        project_t,
        norm_gain,
        norm_bias,
        qkv,
        talk_before,
        talk_after,
        output,
        output_bias,
        mlp_gain,
        mlp_bias,
        hidden,
        depth_two,
        return_t,
        return_bias,
    ) = refs[:WEIGHTS]
    side, code_channels, code_heads, code_units = code_of(codes)
    pixels = (side * side).astype(f32)
    count = images_total * pixels
    live[...] = grid_mask((ROWS, LANES), side)
    half_live[...] = 0.5 * live[...]
    live_d = grid_mask((ROWS, D), side)

    average, inverse = moments(sums[...], count)
    wide_e[...] = jnp.zeros_like(wide_e)
    channel_mask = jnp.where(iota((1, E), 1) < E - (2 - code_channels) * D, 1.0, 0.0)
    wide_e[0:1, :E] = average
    wide_e[1:2, :E] = inverse * gain[...]
    wide_e[2:3, :E] = bias[...]
    wide_e[3:4, :E] = channel_mask
    wide_e[4:13, :E] = depth_one[...] * channel_mask
    wide_e[15:16, :E] = inverse
    tokens = widen(image[...], side).astype(bf16)
    tokens_out[...] = tokens
    token_mean = sums[2:3, :D] / count
    centred_tokens = (tokens.astype(f32) - token_mean) * live_d
    expanded_s[:, E - E % LANES :] = jnp.zeros((ROWS, EP - E + E % LANES), f32)
    expanded_s[:, :E] = dot(tokens, expand[...])

    beside[...] = jnp.zeros_like(beside)
    half_scale[0:1, :] = 0.5 * wide_e[1:2, :]
    half_scale[1:2, :] = 0.5 * (wide_e[2:3, :] - wide_e[0:1, :] * wide_e[1:2, :])

    def forward_one(c, carry):
        at = pl.ds(c * LANES, LANES)
        silu, slope = silu_and_slope(expanded_s[:, at] * half_scale[0:1, at] + half_scale[1:2, at], half_live[...])
        active = silu * live[...]
        active_e[:, at] = active
        slope_e[:, at] = slope
        deep = depthwise(sideways(beside.at[c % 3], active), [wide_e[4 + t : 5 + t, at] for t in range(9)]) * live[...]
        deep_s[:, at] = deep
        wide_e[14:15, at] = row_sum(deep) / pixels
        return carry

    for c in range(EB):
        forward_one(c, 0)
    pooled = wide_e[14:15, :E]
    squeeze_pre = vector_times(pooled, squeeze_t[...], NT) + squeeze_bias[...]
    squeeze_gate = sigmoid(squeeze_pre)
    squeezed = squeeze_pre * squeeze_gate
    excited = sigmoid(vector_times(squeezed, excite[...], ((1,), (0,))) + excite_bias[...])
    wide_e[13:14, :E] = excited
    scaled_s[...] = (deep_s[...] * wide_e[13:14, :]).astype(bf16)
    branch = dot(scaled_s[:, :E], project_t[...], NT)
    handed_low = (tokens.astype(f32) + branch).astype(bf16)
    first_out[...] = narrow(handed_low).astype(bf16)
    handed = handed_low.astype(f32)

    hat_one, rs_one = norm_forward(handed)
    normed_one = (hat_one * norm_gain[...] + norm_bias[...]).astype(bf16)
    projected = dot(normed_one, qkv[...]).astype(bf16).astype(f32)
    live_heads = HEADS - 2 * (2 - code_heads)
    own = jnp.where((iota((HEADS, DP), 1) >= iota((HEADS, DP), 0) * HD), 1.0, 0.0)
    own = jnp.where((iota((HEADS, DP), 1) < iota((HEADS, DP), 0) * HD + HD), own, 0.0)
    own_t = jnp.where((iota((DP, HEADS), 0) >= iota((DP, HEADS), 1) * HD), 1.0, 0.0)
    own_t = jnp.where((iota((DP, HEADS), 0) < iota((DP, HEADS), 1) * HD + HD), own_t, 0.0)
    head_row = jnp.where(iota((1, HEADS), 1) < live_heads, 1.0, 0.0)
    value_mask = jnp.where(iota((1, DP), 1) < live_heads * HD, 1.0, 0.0)
    before = talk_before[...] * head_row * HD ** (-0.5)
    after = talk_after[...] * head_row
    mixes[...] = jnp.zeros_like(mixes)
    mixes[0:HEADS] = dot(before, own, precision=HIGHEST)
    mixes[16 : 16 + HEADS] = dot(after, own, ((0,), (0,)), precision=HIGHEST)
    columns = mixes[...].T
    before_columns = columns[:, 0:16]
    after_columns = columns[:, 16:32]

    three_s[...] = jnp.zeros_like(three_s)
    for which in range(3):
        three_s[which, 0:ROWS, 0:D] = projected[:, which * D : (which + 1) * D]
    three_s[2, 0:ROWS] = three_s[2, 0:ROWS] * value_mask

    spare = iota((ROWS, DP), 1) == D
    row_place = iota((ROWS, DP), 0)
    dead = ((row_place >> 4) >= side) | ((row_place & 15) >= side)
    keys_wide[...] = jnp.where(spare & dead, -1000000000.0, three_s[1, 0:ROWS])
    queries_t = jnp.where(iota((DP, DP), 1) == D, 1.0, three_s[0]).T.astype(bf16)
    queries_twice = jnp.concatenate([queries_t, queries_t], axis=0)
    queries_low = three_s[0].astype(bf16)
    keys_t = three_s[1].T[0:D]
    values_t = three_s[2].T[0:D]
    before_wide = jnp.where(iota((HEADS, DP), 1) == D, 1.0, mixes[0:HEADS] * LOG2E)
    all_soft[:, ROWS:] = jnp.zeros((HEADS, DP - ROWS, DP), bf16)
    all_grad[:, ROWS:] = jnp.zeros((HEADS, DP - ROWS, DP), bf16)
    for h in range(HEADS):
        weighted = keys_wide[...] * before_wide[h : h + 1]
        high = weighted.astype(bf16)
        low = (weighted - high.astype(f32)).astype(bf16)
        scores = dot(jnp.concatenate([high, low], axis=1), queries_twice)
        grown = jnp.exp2(scores - jnp.max(scores, axis=0, keepdims=True))
        soft = grown * (1.0 / row_sum(grown))
        soft_s[h] = soft
        all_soft[h, 0:ROWS] = soft.astype(bf16)
    for h in range(HEADS):
        all_values[:, h * DP : (h + 1) * DP] = (values_t * after_columns[0:D, h : h + 1]).astype(bf16)
    for h in range(HEADS):
        all_keys[:, h * DP : (h + 1) * DP] = (keys_t * before_columns[0:D, h : h + 1]).astype(bf16)
    heads_out_t = dot(all_values[...], all_soft[...].reshape(HEADS * DP, DP))
    heads_out_low = heads_out_t[:, 0:ROWS].astype(bf16)
    heads_out = heads_out_t.T[0:ROWS].astype(bf16)
    attended = dot(heads_out, output[...]) + output_bias[...]
    middle = handed + attended * live_d

    hat_two, rs_two = norm_forward(middle)
    normed_two_f = hat_two * mlp_gain[...] + mlp_bias[...]
    normed_two = normed_two_f.astype(bf16)
    wide_f[...] = jnp.zeros_like(wide_f)
    wide_f[0:1, :F] = hidden_bias[...]
    unit_mask = jnp.where(iota((1, F), 1) < F - (2 - code_units) * D, 1.0, 0.0)
    wide_f[1:2, :F] = unit_mask
    wide_f[2:11, :F] = depth_two[...] * unit_mask
    hidden_s[:, F - F % LANES :] = jnp.zeros((ROWS, FP - F + F % LANES), f32)
    hidden_s[:, :F] = dot(normed_two, hidden[...])

    def forward_two(c, carry):
        at = pl.ds(c * LANES, LANES)
        units = (hidden_s[:, at] + wide_f[0:1, at]) * live[...]
        hidden_s[:, at] = units
        conv = depthwise(sideways(beside.at[c % 3], units), [wide_f[2 + t : 3 + t, at] for t in range(9)]) * live[...]
        silu, slope = silu_and_slope(0.5 * conv, half_live[...])
        slope_s[:, at] = slope
        active_s[:, at] = silu.astype(bf16)
        return carry

    for c in range(FB):
        forward_two(c, 0)
    final = middle + dot(active_s[:, :F], return_t[...], NT) + return_bias[...]
    second_out[...] = narrow((final * live_d).astype(bf16)).astype(bf16)

    upstream = widen(cotangent[...], side)
    grad_return_bias = row_sum(upstream)
    up_s[:, F - F % LANES :] = jnp.zeros((ROWS, FP - F + F % LANES), f32)
    up_s[:, :F] = dot(upstream.astype(bf16), return_t[...])
    smalls_f[...] = jnp.zeros_like(smalls_f)

    def backward_two(c, carry):
        at = pl.ds(c * LANES, LANES)
        three = sideways(beside.at[c % 3], up_s[:, at] * slope_s[:, at])
        taps = depthwise_kernel_grad(three, hidden_s[:, at])
        for t in range(9):
            smalls_f[t : t + 1, at] = taps[t] * wide_f[1:2, at]
        flipped = [wide_f[10 - t : 11 - t, at] for t in range(9)]
        grad_units = depthwise(three, flipped) * live[...]
        smalls_f[9:10, at] = row_sum(grad_units)
        hidden_low_s[:, at] = grad_units.astype(bf16)
        return carry

    for c in range(FB):
        backward_two(c, 0)
    grad_return = dot(upstream.T.astype(bf16), active_s[...])
    for b in range(FB):
        put_block(tiles_out, RETURN + b, block_of(grad_return, b), smalls_f[8:16, b * LANES : (b + 1) * LANES])
    grad_hidden = dot(normed_two_f.T.astype(bf16), hidden_low_s[...])
    for b in range(FB):
        put_block(tiles_out, HIDDEN + b, block_of(grad_hidden, b), smalls_f[0:8, b * LANES : (b + 1) * LANES])
    grad_normed_two = dot(hidden_low_s[:, :F], hidden[...], NT)
    grad_mlp_gain = row_sum(grad_normed_two * hat_two)
    grad_mlp_bias = row_sum(grad_normed_two)
    grad_middle = upstream + norm_backward(grad_normed_two, hat_two, rs_two, mlp_gain[...])

    attend_up = grad_middle * live_d
    grad_output_bias = row_sum(attend_up)
    attend_low = attend_up.astype(bf16)
    grad_output = dot(heads_out_low, attend_low)
    three_s[0] = jnp.zeros((DP, DP), f32)
    three_s[0, 0:ROWS, 0:D] = dot(attend_low, output[...], NT)
    grad_heads_low = three_s[0].astype(bf16)
    grad_heads_t = three_s[0].T.astype(bf16)
    grad_k[...] = jnp.zeros_like(grad_k)
    grad_v[...] = jnp.zeros_like(grad_v)
    weighted = [(three_s[2, 0:ROWS] * mixes[16 + h : 17 + h]).astype(bf16) for h in range(HEADS)]
    grads_soft = dot(jnp.concatenate(weighted, axis=0), grad_heads_t)

    def scores_back(h):
        soft = soft_s[h]
        grad_soft = grads_soft[h * ROWS : (h + 1) * ROWS]
        all_grad[h, 0:ROWS] = (soft * (grad_soft - row_sum(soft * grad_soft))).astype(bf16)

    for h in range(HEADS):
        scores_back(h)
    backs = dot(all_grad[...].reshape(HEADS * DP, DP), queries_low)
    for h in range(HEADS):
        back = backs[h * DP : h * DP + ROWS]
        grad_k[...] += back * mixes[h : h + 1]
        talk_s[h : h + 1, :] = row_sum(back * three_s[1, 0:ROWS])
    backs = dot(all_soft[...].reshape(HEADS * DP, DP), grad_heads_low)
    for h in range(HEADS):
        back = backs[h * DP : h * DP + ROWS]
        grad_v[...] += back * mixes[16 + h : 17 + h]
        talk_s[16 + h : 17 + h, :] = row_sum(back * three_s[2, 0:ROWS])
    grad_q = dot(all_keys[...], all_grad[...].reshape(HEADS * DP, DP)).T[0:ROWS]
    talk_before_grad = dot(talk_s[0:12, :], own_t, precision=HIGHEST) * (head_row * HD ** (-0.5))
    talk_after_grad = dot(own_t, talk_s[16:28, :], ((0,), (1,)), precision=HIGHEST) * head_row
    projected_s[:, :D] = grad_q
    projected_s[:, D : 2 * D] = grad_k[:, :D]
    projected_s[:, 2 * D :] = (grad_v[...] * value_mask)[:, :D]
    grad_projected = projected_s[...].astype(bf16)
    grad_normed_one = dot(grad_projected, qkv[...], NT)
    normed_one_t = (hat_one * norm_gain[...] + norm_bias[...]).T.astype(bf16)
    grad_norm_gain = row_sum(grad_normed_one * hat_one)
    grad_norm_bias = row_sum(grad_normed_one)
    handed_grad = grad_middle + norm_backward(grad_normed_one, hat_one, rs_one, norm_gain[...])
    narrow_into(handed_grad_out, handed_grad)

    talk_s[...] = jnp.zeros_like(talk_s)
    talk_s[0:12, 0:HEADS] = talk_before_grad
    talk_s[16:28, 0:HEADS] = talk_after_grad
    grad_qkv = jnp.concatenate([dot(normed_one_t, grad_projected), jnp.zeros((D, QP - 3 * D), f32)], axis=1)
    for b in range(QB - 1):
        extra = talk_s[8 * b : 8 * b + 8, 0:LANES] if b < 4 else jnp.zeros((8, LANES), f32)
        put_block(tiles_out, QKV + b, block_of(grad_qkv, b), extra)
    talk_s[0:8, :] = jnp.zeros((8, DP), f32)
    talk_s[0:1, :D] = grad_norm_gain
    talk_s[1:2, :D] = grad_norm_bias
    talk_s[2:3, :D] = grad_output_bias
    talk_s[3:4, :D] = grad_mlp_gain
    talk_s[4:5, :D] = grad_mlp_bias
    talk_s[5:6, :D] = grad_return_bias
    leading = lax.axis_index("pipe") == 0
    centred_low = centred_tokens.astype(bf16)
    centred_t = centred_tokens.T.astype(bf16)
    covariance = dot(centred_t, centred_low)
    over = iota((D, D), 0) - iota((D, D), 1)
    over = jnp.where(leading, over, -over)
    talk_s[6:7, :D] = jnp.where(leading, 0.0, row_sum(jnp.where(over == 0, covariance, 0.0)))
    wanted = (over < 0) | ((over == 0) & leading)
    covariance = jnp.concatenate([jnp.where(wanted, covariance, 0.0), jnp.zeros((D, DP - D), f32)], axis=1)
    for b in range(DB):
        put_block(tiles_out, COVARIANCE + b, block_of(covariance, b), jnp.zeros((8, LANES), f32))
    for b in range(DB):
        piece = jnp.concatenate([grad_output, jnp.zeros((D, DP - D), f32)], axis=1)
        extra = talk_s[0:8, :]
        put_block(tiles_out, OUTPUT + b, block_of(piece, b), block_of(extra, b))
    add_tail(tiles_out, QKV_TAIL, block_of(grad_qkv, QB - 1), jnp.zeros((8, LANES), f32))

    back_low = handed_grad.astype(bf16)
    handed_low_out[...] = back_low
    deep_grad[:, E - E % LANES :] = jnp.zeros((ROWS, EP - E + E % LANES), f32)
    deep_grad[:, :E] = dot(back_low, project_t[...])

    excited = wide_e[13:14, :E]
    grad_excited = row_sum(deep_grad[:, :E] * deep_s[:, :E])
    grad_excite_pre = grad_excited * excited * (1.0 - excited)
    grad_squeezed = vector_times(grad_excite_pre, excite[...], NT)
    grad_squeeze_pre = grad_squeezed * (squeeze_gate * (1.0 + squeeze_pre * (1.0 - squeeze_gate)))
    grad_pooled = vector_times(grad_squeeze_pre, squeeze_t[...], ((1,), (0,)))
    factors_out[...] = jnp.zeros_like(factors_out)

    def put_factor(start, row):
        width = row.shape[-1]
        for b in range(-(-width // LANES)):
            end = min(width, (b + 1) * LANES)
            factors_out[start + b : start + b + 1, 0 : end - b * LANES] = row[:, b * LANES : end]

    put_factor(0, wide_e[14:15, :E])
    put_factor(EB, grad_excite_pre)
    put_factor(2 * EB, squeezed)
    put_factor(2 * EB + 3, grad_squeeze_pre)
    wide_e[14:15, :E] = grad_pooled / pixels
    tail_e[...] = jnp.zeros_like(tail_e)
    batch_out[...] = jnp.zeros_like(batch_out)

    def backward_one(c, carry):
        at = pl.ds(c * LANES, LANES)
        grad_deep = (deep_grad[:, at] * wide_e[13:14, at] + wide_e[14:15, at]) * live[...]
        three = sideways(beside.at[c % 3], grad_deep)
        taps = depthwise_kernel_grad(three, active_e[:, at])
        for t in range(8):
            smalls_e[t : t + 1, at] = taps[t] * wide_e[3:4, at]
        flipped = [wide_e[12 - t : 13 - t, at] for t in range(9)]
        grad_normed = depthwise(three, flipped) * slope_e[:, at]
        centred = expanded_s[:, at] - wide_e[0:1, at]
        grad_gain = row_sum(grad_normed * centred) * wide_e[15:16, at]
        grad_bias = row_sum(grad_normed)
        batch_out[pl.ds(c, 1), :] = grad_gain
        batch_out[pl.ds(c + 16, 1), :] = grad_bias
        tail_e[0:1, at] = grad_gain
        tail_e[1:2, at] = grad_bias
        tail_e[2:3, at] = taps[8] * wide_e[3:4, at]
        grad_second = grad_gain * wide_e[15:16, at] * wide_e[1:2, at] * (-1.0 / count)
        tail_e[3:4, at] = jnp.where(leading, grad_second, 0.0)
        tail_e[4:5, at] = jnp.where(leading, 0.0, grad_second)
        expanded_grad_out[:, at] = (grad_normed * wide_e[1:2, at]).astype(bf16)
        return carry

    for c in range(EB):
        backward_one(c, 0)
    grad_project = dot(handed_grad.T.astype(bf16), scaled_s[...])
    for b in range(EB - 1):
        put_block(tiles_out, PROJECT + b, block_of(grad_project, b), smalls_e[:, b * LANES : (b + 1) * LANES])
    add_tail(tiles_out, PROJECT_TAIL, block_of(grad_project, EB - 1), smalls_e[:, EP - LANES :])
    grad_expand = dot(centred_t, expanded_grad_out[...])
    for b in range(EB - 1):
        put_block(tiles_out, EXPAND + b, block_of(grad_expand, b), tail_e[:, b * LANES : (b + 1) * LANES])
    add_tail(tiles_out, EXPAND_TAIL, block_of(grad_expand, EB - 1), tail_e[:, EP - LANES :])
    spare = tiles_out.shape[0] - ALL_TILES
    if spare:
        tiles_out[ALL_TILES:] = jnp.zeros((spare, 16, LANES), bf16)

    half = pieces // 2
    mine = lax.axis_index("pipe")
    base = 0
    for part, order in enumerate(orders):
        size = per_piece[part]
        me = home_of(order) & (half - 1)
        for piece in range(half):
            first = base * 2 + piece * size
            to = pl.ds(base + (piece ^ me) * size, size)
            kept_out[to] = tiles_out[pl.ds(first + mine * half * size, size)]
            sent_out[to] = tiles_out[pl.ds(first + (1 - mine) * half * size, size)]
        base += half * size


RIDE_TILES = 4


def ridden_sum(batch, arrivals):
    total = batch[...].reshape(2, 16, LANES)
    for ref in arrivals:
        end = ref.shape[0]
        total = total + (ref[end - 4 : end - 2].astype(f32) + ref[end - 2 : end].astype(f32))
    return total


def put_ride(ref, total):
    high = total.astype(bf16)
    end = ref.shape[0]
    ref[end - 4 : end - 2] = high
    ref[end - 2 : end] = (total - high.astype(f32)).astype(bf16)


def added(terms, at):
    return functools.reduce(jnp.add, [term[at].astype(f32) for term in terms]).astype(bf16)


def halves_kernel(count, size, rides, *refs):
    if rides:
        own, other, batch, kept, sent, batch_out = refs
        total = ridden_sum(batch, [other] if other.shape[0] > 2 * count * size else [])
        batch_out[...] = total.reshape(batch_out.shape)
        put_ride(sent, total)
    else:
        own, other, kept, sent = refs
    for i in range(count):
        here = slice(i * size, (i + 1) * size)
        there = slice((count + i) * size, (count + i + 1) * size)
        kept[here] = added([own, other], here)
        sent[here] = added([own, other], there)


def pieces_kernel(count, rows, sizes, terms_of, *refs):
    terms = []
    refs = list(refs)
    for number in terms_of:
        terms.append([refs.pop(0) for _ in range(number)])
    batch = refs.pop(0)
    batch_out = refs.pop()
    whole = count * rows * sizes[-1]
    total = ridden_sum(batch, [ref for ref in terms[-1] if ref.shape[0] > whole])
    batch_out[...] = total.reshape(batch_out.shape)
    for j, out in enumerate(refs):
        if j:
            put_ride(out, total)
        for i in range(rows):
            at = i * sum(sizes)
            for part, size in zip(terms, sizes):
                out[at : at + size] = added(part, slice((j * rows + i) * size, (j * rows + i + 1) * size))
                at += size


def finish_kernel(own, *refs):
    *others, batch, factors, held, batch_out = refs
    size = own.shape[0]
    batch_out[...] = ridden_sum(batch, others).reshape(batch_out.shape)
    held[0:size] = added([own, *others], slice(0, size))
    held[size:] = factors[...].astype(bf16).reshape(FACTOR_ROWS // 16, 16, LANES)


def side_by_side_kernel(sizes, *refs):
    outs = refs[len(refs) - len(sizes) :]
    rows = 0
    for ref in refs[: len(refs) - len(sizes)]:
        count = ref.shape[0] // sum(sizes)
        for i in range(count):
            at = i * sum(sizes)
            for out, size in zip(outs, sizes):
                out[rows * size : (rows + 1) * size] = ref[at : at + size]
                at += size
            rows += 1


def last_kernel(
    images_total, codes, sums, total, gain, tokens, handed_low, expanded_grad, expand, grad_out, wide
):
    side = code_of(codes)[0]
    count = images_total * (side * side).astype(f32)
    average, inverse = moments(sums[...], count)
    scale = inverse * gain[...]
    for b in range(EB):
        wide[0:1, b * LANES : (b + 1) * LANES] = total[b : b + 1, :]
        wide[1:2, b * LANES : (b + 1) * LANES] = total[16 + b : 17 + b, :]
    grad_variance = -0.5 * inverse * scale * wide[0:1, :E]
    grad_second = grad_variance / count
    grad_first = (-scale * wide[1:2, :E] - 2.0 * average * grad_variance) / count
    expanded = dot(tokens[...], expand[...])
    grad = (expanded_grad[:, :E].astype(f32) + grad_first + 2.0 * expanded * grad_second).astype(bf16)
    grad_tokens = (handed_low[...].astype(f32) + dot(grad, expand[...], NT)) * grid_mask((ROWS, D), side)
    narrow_into(grad_out, grad_tokens)


def unpack_kernel(pieces, per_piece, orders, merged, *refs):
    expand, *refs = refs
    single = (len(refs) - UNPACKED - merged) // PARTS
    inputs = refs[: merged + PARTS * single]
    (
        expand_out,
        gain_out,
        bias_out,
        depth_one_out,
        squeeze_out,
        squeeze_bias_out,
        excite_out,
        excite_bias_out,
        project_out,
        norm_gain_out,
        norm_bias_out,
        qkv_out,
        talk_before_out,
        talk_after_out,
        output_out,
        output_bias_out,
        mlp_gain_out,
        mlp_bias_out,
        hidden_out,
        hidden_bias_out,
        depth_two_out,
        return_out,
        return_bias_out,
        tiles,
        factors,
        wide,
    ) = refs[merged + PARTS * single :]
    for part, order in enumerate(orders):
        me = home_of(order)
        size = per_piece[part]
        base = sum(per_piece[:part])
        at = 0
        riding = FACTOR_ROWS // 16
        own = inputs[merged + part * single : merged + (part + 1) * single]
        for number, ref in enumerate(inputs[:merged] + own):
            width = sum(per_piece) + riding if number < merged else size + riding * (part == RIDDEN)
            skipped = base if number < merged else 0
            for inner in range(ref.shape[0] // width):
                home = at ^ me
                start = inner * width + skipped
                tiles[pl.ds(base * pieces + home * size, size)] = ref[start : start + size]
                if part == RIDDEN:
                    factor = ref[start + size : start + size + riding]
                    factors[home] = factor.reshape(FACTOR_ROWS, LANES).astype(f32)
                at += 1

    def block(b):
        return tiles[b * TILES : (b + 1) * TILES].reshape(ROWS, LANES).astype(f32)

    def spread(first, count, width, out, take, tail=None):
        for b in range(count):
            value = block(first + b) if b < count - 1 or tail is None else pltpu.roll(block(tail), LANES - TAIL_LANE, 1)
            start, stop = b * LANES, min(width, (b + 1) * LANES)
            out[:, start:stop] = value[0:D, 0 : stop - start]
            for ref, top, row, rows in take:
                if len(ref.shape) == 1:
                    ref[start:stop] = value[D + row, 0 : stop - start]
                else:
                    ref[top : top + rows, start:stop] = value[D + row : D + row + rows, 0 : stop - start]

    spread(PROJECT, EB, E, project_out, [(depth_one_out, 0, 0, 8)], PROJECT_TAIL)
    spread(HIDDEN, FB, F, hidden_out, [(depth_two_out, 0, 0, 8)])
    spread(RETURN, FB, F, return_out, [(depth_two_out, 8, 0, 1), (hidden_bias_out, 0, 1, 1)])
    spread(QKV, QB, 3 * D, qkv_out, [], QKV_TAIL)

    def gathered(start, width):
        columns = [factors[:, start + b, :] for b in range(-(-width // LANES))]
        return jnp.concatenate(columns, axis=1)[:, 0:width]

    pooled = gathered(0, E)
    grad_excite_pre = gathered(EB, E)
    squeezed = gathered(2 * EB, SQ)
    grad_squeeze_pre = gathered(2 * EB + 3, SQ)
    squeeze_out[...] = dot(grad_squeeze_pre.T.astype(bf16), pooled.astype(bf16))
    excite_out[...] = dot(squeezed.T.astype(bf16), grad_excite_pre.astype(bf16))
    squeeze_bias_out[...] = jnp.sum(grad_squeeze_pre, axis=0)
    excite_bias_out[...] = jnp.sum(grad_excite_pre, axis=0)

    tail = pltpu.roll(block(EXPAND_TAIL), LANES - TAIL_LANE, 1)
    for b in range(EB):
        value = block(EXPAND + b) if b < EB - 1 else tail
        wide[:, b * LANES : (b + 1) * LANES] = value
    gain_out[...] = wide[D, 0:E]
    bias_out[...] = wide[D + 1, 0:E]
    depth_one_out[8:9, :] = wide[D + 2 : D + 3, 0:E]
    both = jnp.concatenate([block(COVARIANCE), block(COVARIANCE + 1)], axis=1)[0:D, 0:D]
    turned = both.T
    over = iota((D, D), 0) - iota((D, D), 1)
    diagonal = jnp.concatenate([block(OUTPUT)[D + 6 : D + 7], block(OUTPUT + 1)[D + 6 : D + 7]], axis=1)[:, 0:D]
    first = jnp.where(over <= 0, both, turned).astype(bf16)
    second = jnp.where(over > 0, both, jnp.where(over < 0, turned, diagonal)).astype(bf16)
    added = dot(first, expand[...]) * wide[D + 3 : D + 4, 0:E] + dot(second, expand[...]) * wide[D + 4 : D + 5, 0:E]
    expand_out[...] = wide[0:D, 0:E] + added
    vectors = (norm_gain_out, norm_bias_out, output_bias_out, mlp_gain_out, mlp_bias_out, return_bias_out)
    spread(OUTPUT, DB, D, output_out, [(ref, 0, row, 1) for row, ref in enumerate(vectors)])
    talk_before_out[0:8] = block(QKV)[D : D + 8, 0:HEADS]
    talk_before_out[8:12] = block(QKV + 1)[D : D + 4, 0:HEADS]
    talk_after_out[0:8] = block(QKV + 2)[D : D + 8, 0:HEADS]
    talk_after_out[8:12] = block(QKV + 3)[D : D + 4, 0:HEADS]

def kernel_call(body, name, shapes, scratch, operands, fetched, limit, flops):
    in_specs = [pl.BlockSpec(memory_space=pltpu.VMEM)] * len(operands)
    if fetched is not None:
        in_specs[0] = pl.BlockSpec(memory_space=pltpu.SMEM)
        in_specs += [pl.BlockSpec(memory_space=pltpu.HBM)] * len(fetched)
    return pl.pallas_call(
        body,
        out_shape=[jax.ShapeDtypeStruct(shape, kind) for shape, kind in shapes],
        in_specs=in_specs,
        out_specs=[pl.BlockSpec(memory_space=pltpu.VMEM)] * len(shapes),
        scratch_shapes=scratch,
        compiler_params=pltpu.CompilerParams(vmem_limit_bytes=limit * MIB),
        cost_estimate=pl.CostEstimate(flops=flops, bytes_accessed=8 * MIB, transcendentals=0),
        name=name,
    )(*operands, *(fetched or ()))


def swapped(value, axis, mask):
    size = lax.axis_size(axis)
    return lax.ppermute(value, axis, [(i, i ^ mask) for i in range(size)])


def summed_over_dp(value, bits):
    for first in range(0, bits, 2):
        here = [1 << b for b in range(first, min(first + 2, bits))]
        masks = here + ([here[0] | here[1]] if len(here) == 2 else [])
        others = [swapped(value, "dp", mask) for mask in masks]
        value = value + functools.reduce(jnp.add, others)
    return value


def on_device(
    images,
    codes,
    cotangent,
    expand_weight,
    batch_gain,
    batch_bias,
    depth_one,
    squeeze_weight,
    squeeze_bias,
    excite_weight,
    excite_bias,
    project_weight,
    norm_gain,
    norm_bias,
    qkv_weight,
    talk_before,
    talk_after,
    output_weight,
    output_bias,
    mlp_gain,
    mlp_bias,
    hidden_weight,
    hidden_bias,
    depth_two,
    return_weight,
    return_bias,
):
    devices_dp = lax.axis_size("dp")
    bits = devices_dp.bit_length() - 1
    pieces = 2 * devices_dp
    half = pieces // 2
    images_total = float(images.shape[1] * devices_dp)
    per_piece = -(-ALL_TILES // pieces)
    per_piece = [per_piece - per_piece // 2, per_piece // 2]
    factor_tiles = FACTOR_ROWS // 16
    pipe = lax.axis_index("pipe")

    rest = list(range(2, bits))
    groups = [rest[g : g + 2] for g in range(0, len(rest), 2)]
    orders = [[1, 0] + rest, [0, 1] + rest]
    image = lax.dynamic_index_in_dim(images, pipe, 0, keepdims=False)[0]
    upstream = lax.dynamic_index_in_dim(cotangent, pipe, 0, keepdims=False)[0]

    def row(vector):
        return vector.reshape(1, -1)

    def buffers(arrays):
        return [pltpu.VMEM(a.shape, a.dtype) for a in arrays]

    squeeze_t = squeeze_weight.T
    project_t = project_weight.T
    return_t = return_weight.T
    gain = row(batch_gain)

    (sums,) = kernel_call(
        sums_kernel,
        "sums",
        [((3, E), f32)],
        buffers([expand_weight]) + [pltpu.SemaphoreType.DMA((1,))],
        (codes, image),
        (expand_weight,),
        16,
        1 << 33,
    )
    sums = summed_over_dp(sums, bits)

    operands = (
        codes,
        image,
        upstream,
        sums,
        gain,
        row(batch_bias),
        row(squeeze_bias),
        row(excite_bias),
        row(hidden_bias),
        expand_weight,
        depth_one,
        squeeze_t,
        excite_weight,
        project_t,
        row(norm_gain),
        row(norm_bias),
        qkv_weight,
        talk_before,
        talk_after,
        output_weight,
        row(output_bias),
        row(mlp_gain),
        row(mlp_bias),
        hidden_weight,
        depth_two,
        return_t,
        row(return_bias),
    )
    shapes = [
        ((PIX, D), bf16),
        ((PIX, D), bf16),
        ((PIX, D), f32),
        ((ROWS, D), bf16),
        ((ROWS, D), bf16),
        ((ROWS, EP), bf16),
        ((32, LANES), f32),
        ((sum(per_piece) * half, 16, LANES), bf16),
        ((sum(per_piece) * half, 16, LANES), bf16),
        ((FACTOR_ROWS, LANES), f32),
    ]
    scratch = [
        pltpu.VMEM((sum(per_piece) * pieces, 16, LANES), bf16),
        pltpu.VMEM((16, EP), f32),
        pltpu.VMEM((16, FP), f32),
        pltpu.VMEM((ROWS, LANES), f32),
        pltpu.VMEM((ROWS, LANES), f32),
        pltpu.VMEM((3, ROWS + 16, LANES), f32),
        pltpu.VMEM((8, EP), f32),
        pltpu.VMEM((ROWS, EP), f32),
        pltpu.VMEM((ROWS, EP), f32),
        pltpu.VMEM((ROWS, EP), f32),
        pltpu.VMEM((ROWS, EP), f32),
        pltpu.VMEM((ROWS, EP), f32),
        pltpu.VMEM((ROWS, EP), bf16),
        pltpu.VMEM((32, DP), f32),
        pltpu.VMEM((3, DP, DP), f32),
        pltpu.VMEM((ROWS, DP), f32),
        pltpu.VMEM((HEADS, ROWS, DP), f32),
        pltpu.VMEM((HEADS, DP, DP), bf16),
        pltpu.VMEM((HEADS, DP, DP), bf16),
        pltpu.VMEM((D, HEADS * DP), bf16),
        pltpu.VMEM((D, HEADS * DP), bf16),
        pltpu.VMEM((ROWS, FP), f32),
        pltpu.VMEM((ROWS, FP), f32),
        pltpu.VMEM((ROWS, FP), bf16),
        pltpu.VMEM((ROWS, FP), bf16),
        pltpu.VMEM((ROWS, FP), f32),
        pltpu.VMEM((8, EP), f32),
        pltpu.VMEM((8, EP), f32),
        pltpu.VMEM((16, FP), f32),
        pltpu.VMEM((ROWS, DP), f32),
        pltpu.VMEM((ROWS, DP), f32),
        pltpu.VMEM((32, DP), f32),
        pltpu.VMEM((ROWS, 3 * D), f32),
    ]
    first, second, handed_grad, handed_low, tokens, expanded_grad, batch, kept, sent, factors = kernel_call(
        functools.partial(middle_kernel, images_total, pieces, per_piece, orders),
        "middle",
        shapes,
        scratch,
        operands,
        (),
        40,
        1 << 32,
    )

    def masks_of(group):
        return [sum(1 << b for i, b in enumerate(group) if (j >> (len(group) - 1 - i)) & 1) for j in range(1 << len(group))]

    def tiles_of(count):
        return ((count, 16, LANES), bf16)

    def small_kernel(body, name, shapes, operands):
        return kernel_call(body, name, shapes, [], operands, None, 2, 1 << 20)

    arrived = swapped(sent, "pipe", 1)
    cuts = [0, half * per_piece[0], half * sum(per_piece)]
    terms = [[value[cuts[part] : cuts[part + 1]] for value in (kept, arrived)] for part in range(PARTS)]
    held = [None] * PARTS
    count = half
    for step in range(2):
        count //= 2
        for part, order in enumerate(orders):
            size = per_piece[part]
            rides = part == RIDDEN
            body = functools.partial(halves_kernel, count, size, rides)
            shapes = [tiles_of(count * size), tiles_of(count * size + RIDE_TILES * rides)]
            if rides:
                mine, going, batch = small_kernel(body, "halves", shapes + [((32, LANES), f32)], (*terms[part], batch))
            else:
                mine, going = small_kernel(body, "halves", shapes, terms[part])
            held[part] = (mine, swapped(going, "dp", 1 << order[step]))
        terms = [list(pair) for pair in held]
    sizes = per_piece
    for group in groups:
        masks = masks_of(group)
        count //= len(masks)
        body = functools.partial(pieces_kernel, len(masks), count, sizes, [len(part) for part in terms])
        shapes = [tiles_of(count * sum(sizes) + (RIDE_TILES if j else 0)) for j in range(len(masks))]
        *going, batch = small_kernel(
            body, "pieces", shapes + [((32, LANES), f32)], (*[term for part in terms for term in part], batch)
        )
        sizes = [sum(sizes)]
        terms = [[going[0]] + [swapped(value, "dp", mask) for value, mask in zip(going[1:], masks[1:])]]
    held, batch = small_kernel(
        finish_kernel, "finish", [tiles_of(sum(sizes) + factor_tiles), ((32, LANES), f32)], (*terms[0], batch, factors)
    )
    (images_grad,) = kernel_call(
        functools.partial(last_kernel, images_total),
        "last",
        [((PIX, D), f32)],
        [pltpu.VMEM((2, EP), f32)],
        (codes, sums, batch, gain, tokens, handed_low, expanded_grad, expand_weight),
        (),
        16,
        1 << 31,
    )

    sizes = [per_piece[0], per_piece[1] + factor_tiles]
    merged = [held]
    for number, group in enumerate(reversed(groups)):
        merged += [swapped(held, "dp", mask) for mask in masks_of(group)[1:]]
        count *= 1 << len(group)
        if number < len(groups) - 1:
            (held,) = small_kernel(
                functools.partial(side_by_side_kernel, [sum(sizes)]), "together", [tiles_of(count * sum(sizes))], merged
            )
    held = list(
        small_kernel(
            functools.partial(side_by_side_kernel, sizes), "apart", [tiles_of(count * size) for size in sizes], merged
        )
    )
    held, images_grad = lax.optimization_barrier((held, images_grad))
    held = list(held)

    leading = pipe == 0

    def both_layers(one, two):
        other = swapped(jnp.where(leading, two, one), "pipe", 1)
        return jnp.where(leading, jnp.stack([one, other]), jnp.stack([other, two]))[None, :, None]

    activations = both_layers(first, second)
    input_grads = both_layers(images_grad, handed_grad)
    collected = [[], []]
    for step in (1, 0):
        arrived = [swapped(value, "dp", 1 << order[step]) for value, order in zip(held[::-1], orders[::-1])][::-1]
        count *= 2
        for part, size in enumerate(sizes):
            collected[part].append(arrived[part])
            (held[part],) = small_kernel(
                functools.partial(side_by_side_kernel, [size]),
                "together",
                [tiles_of(count * size)],
                (held[part], arrived[part]),
            )
    held, activations, input_grads = lax.optimization_barrier((held, activations, input_grads))
    for part in range(PARTS):
        collected[part].append(swapped(held[part], "pipe", 1))
    grads = kernel_call(
        functools.partial(unpack_kernel, pieces, per_piece, orders, len(merged)),
        "unpack",
        [
            ((D, E), f32),
            ((E,), f32),
            ((E,), f32),
            ((9, E), f32),
            ((SQ, E), f32),
            ((SQ,), f32),
            ((SQ, E), f32),
            ((E,), f32),
            ((D, E), f32),
            ((D,), f32),
            ((D,), f32),
            ((D, 3 * D), f32),
            ((HEADS, HEADS), f32),
            ((HEADS, HEADS), f32),
            ((D, D), f32),
            ((D,), f32),
            ((D,), f32),
            ((D,), f32),
            ((D, F), f32),
            ((F,), f32),
            ((9, F), f32),
            ((D, F), f32),
            ((D,), f32),
        ],
        [
            pltpu.VMEM((sum(per_piece) * pieces, 16, LANES), bf16),
            pltpu.VMEM((pieces, FACTOR_ROWS, LANES), f32),
            pltpu.VMEM((ROWS, EP), f32),
        ],
        (expand_weight, *merged, *collected[0], *collected[1]),
        None,
        40,
        1 << 26,
    )
    grads = list(grads)
    for transposed in (4, 8, 21):
        grads[transposed] = grads[transposed].T

    return (activations, input_grads, *grads)


def solution(mesh):
    in_specs = (P(None, "dp", None, None), P(), P(None, "dp", None, None)) + (P(),) * 23
    out_specs = (P("pipe", None, "dp", None, None), P("pipe", None, "dp", None, None)) + (P(),) * 23
    return jax.shard_map(on_device, mesh=mesh, in_specs=in_specs, out_specs=out_specs, check_vma=False)
```

```python
import functools
import math

import jax
import jax.numpy as jnp
from jax import lax
from jax.experimental import pallas as pl
from jax.experimental.layout import Layout, with_layout_constraint
from jax.experimental.pallas import tpu as pltpu
from jax.sharding import PartitionSpec as P

D = 216
E = 1296
SQ = 324
HEADS = 12
HD = 18
F = 864
SIDE = 14
PIX = 196
EPSILON = 1e-05
LOG2E = 1.4426950408889634

WIDE = 16
ROWS = SIDE * WIDE
LANES = 128
EB = -(-E // LANES)
FB = -(-F // LANES)
DB = -(-D // LANES)
EP = EB * LANES
FP = FB * LANES
DP = DB * LANES
QB = -(-3 * D // LANES)
QP = QB * LANES

PROJECT = 0
HIDDEN = PROJECT + EB - 1
RETURN = HIDDEN + FB
QKV = RETURN + FB
OUTPUT = QKV + QB - 1
COVARIANCE = OUTPUT + DB
EXPAND = COVARIANCE + DB
BLOCKS = EXPAND + EB - 1
PROJECT_TAIL = HIDDEN + FB - 1
EXPAND_TAIL = RETURN + FB - 1
QKV_TAIL = OUTPUT + DB - 1
TAIL_LANE = 96
TILES = ROWS // 16
ALL_TILES = BLOCKS * TILES
PARTS = 2
RIDDEN = 1
FACTOR_ROWS = 32
WEIGHTS = 17
UNPACKED = 26

f32 = jnp.float32
bf16 = jnp.bfloat16
HIGHEST = lax.Precision.HIGHEST
MIB = 1 << 20


def dot(a, b, contract=((1,), (0,)), precision=None):
    return lax.dot_general(a, b, (contract, ((), ())), preferred_element_type=f32, precision=precision)


NT = ((1,), (1,))


def iota(shape, dim):
    return lax.broadcasted_iota(jnp.int32, shape, dim)


def sigmoid(v):
    return 0.5 * jnp.tanh(0.5 * v) + 0.5


def silu_and_slope(half, live):
    turn = jnp.tanh(half)
    more = 1.0 + turn
    return half * more, (more * (1.0 + half * (1.0 - turn))) * live


def grid_mask(shape, side):
    row = iota(shape, 0)
    return jnp.where(((row >> 4) < side) & ((row & 15) < side), 1.0, 0.0)


def widen(tokens, side):
    row = iota((ROWS, PIX), 0)
    hit = iota((ROWS, PIX), 1) == (row >> 4) * SIDE + (row & 15)
    pick = jnp.where(hit & ((row >> 4) < side) & ((row & 15) < side), 1.0, 0.0).astype(bf16)
    return dot(pick, tokens)


def narrow(tokens):
    column = iota((PIX, ROWS), 1)
    hit = iota((PIX, ROWS), 0) == (column >> 4) * SIDE + (column & 15)
    pick = jnp.where(hit & ((column & 15) < SIDE), 1.0, 0.0).astype(bf16)
    return dot(pick, tokens)


def narrow_into(ref, tokens):
    for i in range(SIDE):
        ref[i * SIDE : (i + 1) * SIDE, :] = tokens[i * WIDE : i * WIDE + SIDE, :]


def grid(v):
    return v.reshape(SIDE, WIDE, v.shape[-1])


def flat(v):
    return v.reshape(ROWS, v.shape[-1])


def sideways(ref, v):
    ref[8 : 8 + ROWS] = v
    return [ref[7 : 7 + ROWS], v, ref[9 : 9 + ROWS]]


def depthwise(three, kernel):
    rows = [sum(kernel[3 * a + b] * three[b] for b in range(3)) for a in range(3)]
    zero = jnp.zeros((1, WIDE, LANES), f32)
    above = flat(jnp.concatenate([zero, grid(rows[0])[:-1]], axis=0))
    below = flat(jnp.concatenate([grid(rows[2])[1:], zero], axis=0))
    return rows[1] + above + below


def depthwise_kernel_grad(three, v):
    v3 = grid(v.astype(bf16))
    sides = [grid(side.astype(bf16)) for side in three]
    row = jnp.zeros((1, WIDE, LANES), bf16)
    products = []
    for a in (-1, 0, 1):
        for b in (-1, 0, 1):
            g3 = sides[1 - b]
            if a < 0:
                product = jnp.concatenate([v3[:-1] * g3[1:], row], axis=0)
            elif a > 0:
                product = jnp.concatenate([v3[1:] * g3[:-1], row], axis=0)
            else:
                product = v3 * g3
            products.append(flat(product))
    sums = dot(jnp.ones((16, ROWS), bf16), jnp.concatenate(products, axis=1))
    return [sums[0:1, t * LANES : (t + 1) * LANES] for t in range(9)]


def norm_forward(v):
    centred = v - jnp.sum(v, axis=-1, keepdims=True) * (1.0 / D)
    rs = lax.rsqrt(jnp.sum(centred * centred, axis=-1, keepdims=True) * (1.0 / D) + EPSILON)
    return centred * rs, rs


def norm_backward(grad, hat, rs, gain):
    scaled = grad * gain
    first = jnp.sum(scaled, axis=-1, keepdims=True) * (1.0 / D)
    second = jnp.sum(scaled * hat, axis=-1, keepdims=True) * (1.0 / D)
    return rs * (scaled - first - hat * second)


def row_sum(v):
    return jnp.sum(v, axis=0, keepdims=True)


def vector_times(row, matrix, contract):
    high = row.astype(bf16).astype(f32)
    rest = row - high
    mid = rest.astype(bf16).astype(f32)
    low = rest - mid
    which = iota((16, row.shape[-1]), 0)
    stack = jnp.where(which == 0, high, jnp.where(which == 1, mid, jnp.where(which == 2, low, 0.0)))
    return row_sum(dot(stack.astype(bf16), matrix, contract))


def moments(sums, count):
    average = sums[0:1] / count
    variance = sums[1:2] / count - average * average
    return average, lax.rsqrt(variance + EPSILON)


def put_block(tiles_ref, block, grad, smalls):
    tiles_ref[block * TILES : (block + 1) * TILES] = (
        jnp.concatenate([grad, smalls], axis=0).astype(bf16).reshape(TILES, 16, LANES)
    )


def add_tail(tiles_ref, block, grad, smalls):
    at = slice(block * TILES, (block + 1) * TILES)
    tail = pltpu.roll(jnp.concatenate([grad, smalls], axis=0), TAIL_LANE, 1)
    held = tiles_ref[at].reshape(ROWS, LANES).astype(f32)
    tiles_ref[at] = (held + tail).astype(bf16).reshape(TILES, 16, LANES)


def block_of(v, b):
    return v[:, b * LANES : (b + 1) * LANES]


def code_of(codes):
    mine = lax.axis_index("pipe")
    return SIDE - 4 + 2 * codes[mine, 3], codes[mine, 0], codes[mine, 1], codes[mine, 2]


def home_of(order):
    spot = lax.axis_index("dp")
    home = lax.axis_index("pipe")
    for b in order:
        home = home * 2 + ((spot >> b) & 1)
    return home


def fetch(sources, targets, sems):
    copies = [pltpu.make_async_copy(a, b, sems.at[i]) for i, (a, b) in enumerate(zip(sources, targets))]
    for copy in copies:
        copy.start()
    return copies


def sums_kernel(image, expand_hbm, codes_hbm, sums_out, tokens_out, expanded_out, expand, codes, sems):
    expand_copy, codes_copy = fetch([expand_hbm, codes_hbm], [expand, codes], sems)
    tokens = widen(image[...], SIDE).astype(bf16)
    expand_copy.wait()
    expanded = dot(tokens, expand[...])
    codes_copy.wait()
    live = grid_mask((ROWS, 1), code_of(codes)[0])
    tokens = tokens.astype(f32) * live
    expanded = expanded * live
    tokens_out[...] = tokens.astype(bf16)
    expanded_out[:, E - E % LANES :] = jnp.zeros((ROWS, EP - E + E % LANES), f32)
    expanded_out[:, :E] = expanded
    sums_out[0:1, :] = row_sum(expanded)
    sums_out[1:2, :] = row_sum(expanded * expanded)
    sums_out[2:3, :] = jnp.zeros((1, E), f32)
    sums_out[2:3, :D] = row_sum(tokens)


def middle_kernel(
    images_total,
    pieces,
    per_piece,
    orders,
    codes,
    tokens_in,
    expanded_s,
    cotangent,
    sums,
    gain,
    bias,
    squeeze_bias,
    excite_bias,
    hidden_bias,
    *refs,
):
    (
        first_out,
        second_out,
        handed_grad_out,
        handed_low_out,
        expanded_grad_out,
        batch_out,
        kept_low,
        kept_high,
        sent_low,
        sent_high,
        factors_out,
        tiles_out,
        wide_e,
        wide_f,
        live,
        half_live,
        beside,
        half_scale,
        deep_grad,
        active_e,
        slope_e,
        deep_s,
        scaled_s,
        mixes,
        three_s,
        keys_wide,
        soft_s,
        all_soft,
        all_grad,
        all_keys,
        all_values,
        hidden_s,
        slope_s,
        active_s,
        hidden_low_s,
        up_s,
        smalls_e,
        tail_e,
        smalls_f,
        grad_k,
        grad_v,
        talk_s,
        projected_s,
    ) = refs[WEIGHTS:]
    (
        depth_one,
        squeeze_t,
        excite,
        project_t,
        norm_gain,
        norm_bias,
        qkv,
        talk_before,
        talk_after,
        output,
        output_bias,
        mlp_gain,
        mlp_bias,
        hidden,
        depth_two,
        return_t,
        return_bias,
    ) = refs[:WEIGHTS]
    side, code_channels, code_heads, code_units = code_of(codes)
    pixels = (side * side).astype(f32)
    count = images_total * pixels
    live[...] = grid_mask((ROWS, LANES), side)
    half_live[...] = 0.5 * live[...]
    live_d = grid_mask((ROWS, D), side)

    average, inverse = moments(sums[...], count)
    wide_e[...] = jnp.zeros_like(wide_e)
    channel_mask = jnp.where(iota((1, E), 1) < E - (2 - code_channels) * D, 1.0, 0.0)
    wide_e[0:1, :E] = average
    wide_e[1:2, :E] = inverse * gain[...]
    wide_e[2:3, :E] = bias[...]
    wide_e[3:4, :E] = channel_mask
    wide_e[4:13, :E] = depth_one[...] * channel_mask
    wide_e[15:16, :E] = inverse
    tokens = tokens_in[...]
    token_mean = sums[2:3, :D] / count
    centred_tokens = (tokens.astype(f32) - token_mean) * live_d

    beside[...] = jnp.zeros_like(beside)
    half_scale[0:1, :] = 0.5 * wide_e[1:2, :]
    half_scale[1:2, :] = 0.5 * (wide_e[2:3, :] - wide_e[0:1, :] * wide_e[1:2, :])

    def forward_one(c, carry):
        at = pl.ds(c * LANES, LANES)
        silu, slope = silu_and_slope(expanded_s[:, at] * half_scale[0:1, at] + half_scale[1:2, at], half_live[...])
        active = silu * live[...]
        active_e[:, at] = active
        slope_e[:, at] = slope
        deep = depthwise(sideways(beside.at[c % 3], active), [wide_e[4 + t : 5 + t, at] for t in range(9)]) * live[...]
        deep_s[:, at] = deep
        wide_e[14:15, at] = row_sum(deep) / pixels
        return carry

    for c in range(EB):
        forward_one(c, 0)
    pooled = wide_e[14:15, :E]
    squeeze_pre = vector_times(pooled, squeeze_t[...], NT) + squeeze_bias[...]
    squeeze_gate = sigmoid(squeeze_pre)
    squeezed = squeeze_pre * squeeze_gate
    excited = sigmoid(vector_times(squeezed, excite[...], ((1,), (0,))) + excite_bias[...])
    wide_e[13:14, :E] = excited
    scaled_s[...] = (deep_s[...] * wide_e[13:14, :]).astype(bf16)
    branch = dot(scaled_s[:, :E], project_t[...], NT)
    handed_low = (tokens.astype(f32) + branch).astype(bf16)
    first_out[...] = narrow(handed_low).astype(bf16)
    handed = handed_low.astype(f32)

    hat_one, rs_one = norm_forward(handed)
    normed_one = (hat_one * norm_gain[...] + norm_bias[...]).astype(bf16)
    projected = dot(normed_one, qkv[...]).astype(bf16).astype(f32)
    live_heads = HEADS - 2 * (2 - code_heads)
    own = jnp.where((iota((HEADS, DP), 1) >= iota((HEADS, DP), 0) * HD), 1.0, 0.0)
    own = jnp.where((iota((HEADS, DP), 1) < iota((HEADS, DP), 0) * HD + HD), own, 0.0)
    own_t = jnp.where((iota((DP, HEADS), 0) >= iota((DP, HEADS), 1) * HD), 1.0, 0.0)
    own_t = jnp.where((iota((DP, HEADS), 0) < iota((DP, HEADS), 1) * HD + HD), own_t, 0.0)
    head_row = jnp.where(iota((1, HEADS), 1) < live_heads, 1.0, 0.0)
    value_mask = jnp.where(iota((1, DP), 1) < live_heads * HD, 1.0, 0.0)
    before = talk_before[...] * head_row * HD ** (-0.5)
    after = talk_after[...] * head_row
    mixes[...] = jnp.zeros_like(mixes)
    mixes[0:HEADS] = dot(before, own, precision=HIGHEST)
    mixes[16 : 16 + HEADS] = dot(after, own, ((0,), (0,)), precision=HIGHEST)
    columns = mixes[...].T
    before_columns = columns[:, 0:16]
    after_columns = columns[:, 16:32]

    three_s[...] = jnp.zeros_like(three_s)
    for which in range(3):
        three_s[which, 0:ROWS, 0:D] = projected[:, which * D : (which + 1) * D]
    three_s[2, 0:ROWS] = three_s[2, 0:ROWS] * value_mask

    spare = iota((ROWS, DP), 1) == D
    row_place = iota((ROWS, DP), 0)
    dead = ((row_place >> 4) >= side) | ((row_place & 15) >= side)
    keys_wide[...] = jnp.where(spare & dead, -1000000000.0, three_s[1, 0:ROWS])
    queries_t = jnp.where(iota((DP, DP), 1) == D, 1.0, three_s[0]).T.astype(bf16)
    queries_twice = jnp.concatenate([queries_t, queries_t], axis=0)
    queries_low = three_s[0].astype(bf16)
    keys_t = three_s[1].T[0:D]
    values_t = three_s[2].T[0:D]
    before_wide = jnp.where(iota((HEADS, DP), 1) == D, 1.0, mixes[0:HEADS] * LOG2E)
    all_soft[:, ROWS:] = jnp.zeros((HEADS, DP - ROWS, DP), bf16)
    all_grad[:, ROWS:] = jnp.zeros((HEADS, DP - ROWS, DP), bf16)
    for h in range(HEADS):
        weighted = keys_wide[...] * before_wide[h : h + 1]
        high = weighted.astype(bf16)
        low = (weighted - high.astype(f32)).astype(bf16)
        scores = dot(jnp.concatenate([high, low], axis=1), queries_twice)
        grown = jnp.exp2(scores - jnp.max(scores, axis=0, keepdims=True))
        soft = grown * (1.0 / row_sum(grown))
        soft_s[h] = soft
        all_soft[h, 0:ROWS] = soft.astype(bf16)
    for h in range(HEADS):
        all_values[:, h * DP : (h + 1) * DP] = (values_t * after_columns[0:D, h : h + 1]).astype(bf16)
    for h in range(HEADS):
        all_keys[:, h * DP : (h + 1) * DP] = (keys_t * before_columns[0:D, h : h + 1]).astype(bf16)
    heads_out_t = dot(all_values[...], all_soft[...].reshape(HEADS * DP, DP))
    heads_out_low = heads_out_t[:, 0:ROWS].astype(bf16)
    heads_out = heads_out_t.T[0:ROWS].astype(bf16)
    attended = dot(heads_out, output[...]) + output_bias[...]
    middle = handed + attended * live_d

    hat_two, rs_two = norm_forward(middle)
    normed_two_f = hat_two * mlp_gain[...] + mlp_bias[...]
    normed_two = normed_two_f.astype(bf16)
    wide_f[...] = jnp.zeros_like(wide_f)
    wide_f[0:1, :F] = hidden_bias[...]
    unit_mask = jnp.where(iota((1, F), 1) < F - (2 - code_units) * D, 1.0, 0.0)
    wide_f[1:2, :F] = unit_mask
    wide_f[2:11, :F] = depth_two[...] * unit_mask
    hidden_s[:, F - F % LANES :] = jnp.zeros((ROWS, FP - F + F % LANES), f32)
    hidden_s[:, :F] = dot(normed_two, hidden[...])

    def forward_two(c, carry):
        at = pl.ds(c * LANES, LANES)
        units = (hidden_s[:, at] + wide_f[0:1, at]) * live[...]
        hidden_s[:, at] = units
        conv = depthwise(sideways(beside.at[c % 3], units), [wide_f[2 + t : 3 + t, at] for t in range(9)]) * live[...]
        silu, slope = silu_and_slope(0.5 * conv, half_live[...])
        slope_s[:, at] = slope
        active_s[:, at] = silu.astype(bf16)
        return carry

    for c in range(FB):
        forward_two(c, 0)
    final = middle + dot(active_s[:, :F], return_t[...], NT) + return_bias[...]
    second_out[...] = narrow((final * live_d).astype(bf16)).astype(bf16)

    upstream = widen(cotangent[...], side)
    grad_return_bias = row_sum(upstream)
    up_s[:, F - F % LANES :] = jnp.zeros((ROWS, FP - F + F % LANES), f32)
    up_s[:, :F] = dot(upstream.astype(bf16), return_t[...])
    smalls_f[...] = jnp.zeros_like(smalls_f)

    def backward_two(c, carry):
        at = pl.ds(c * LANES, LANES)
        three = sideways(beside.at[c % 3], up_s[:, at] * slope_s[:, at])
        taps = depthwise_kernel_grad(three, hidden_s[:, at])
        for t in range(9):
            smalls_f[t : t + 1, at] = taps[t] * wide_f[1:2, at]
        flipped = [wide_f[10 - t : 11 - t, at] for t in range(9)]
        grad_units = depthwise(three, flipped) * live[...]
        smalls_f[9:10, at] = row_sum(grad_units)
        hidden_low_s[:, at] = grad_units.astype(bf16)
        return carry

    for c in range(FB):
        backward_two(c, 0)
    grad_return = dot(upstream.T.astype(bf16), active_s[...])
    for b in range(FB):
        put_block(tiles_out, RETURN + b, block_of(grad_return, b), smalls_f[8:16, b * LANES : (b + 1) * LANES])
    grad_hidden = dot(normed_two_f.T.astype(bf16), hidden_low_s[...])
    for b in range(FB):
        put_block(tiles_out, HIDDEN + b, block_of(grad_hidden, b), smalls_f[0:8, b * LANES : (b + 1) * LANES])
    grad_normed_two = dot(hidden_low_s[:, :F], hidden[...], NT)
    grad_mlp_gain = row_sum(grad_normed_two * hat_two)
    grad_mlp_bias = row_sum(grad_normed_two)
    grad_middle = upstream + norm_backward(grad_normed_two, hat_two, rs_two, mlp_gain[...])

    attend_up = grad_middle * live_d
    grad_output_bias = row_sum(attend_up)
    attend_low = attend_up.astype(bf16)
    grad_output = dot(heads_out_low, attend_low)
    three_s[0] = jnp.zeros((DP, DP), f32)
    three_s[0, 0:ROWS, 0:D] = dot(attend_low, output[...], NT)
    grad_heads_low = three_s[0].astype(bf16)
    grad_heads_t = three_s[0].T.astype(bf16)
    grad_k[...] = jnp.zeros_like(grad_k)
    grad_v[...] = jnp.zeros_like(grad_v)
    weighted = [(three_s[2, 0:ROWS] * mixes[16 + h : 17 + h]).astype(bf16) for h in range(HEADS)]
    grads_soft = dot(jnp.concatenate(weighted, axis=0), grad_heads_t)

    def scores_back(h):
        soft = soft_s[h]
        grad_soft = grads_soft[h * ROWS : (h + 1) * ROWS]
        all_grad[h, 0:ROWS] = (soft * (grad_soft - row_sum(soft * grad_soft))).astype(bf16)

    for h in range(HEADS):
        scores_back(h)
    backs = dot(all_grad[...].reshape(HEADS * DP, DP), queries_low)
    for h in range(HEADS):
        back = backs[h * DP : h * DP + ROWS]
        grad_k[...] += back * mixes[h : h + 1]
        talk_s[h : h + 1, :] = row_sum(back * three_s[1, 0:ROWS])
    backs = dot(all_soft[...].reshape(HEADS * DP, DP), grad_heads_low)
    for h in range(HEADS):
        back = backs[h * DP : h * DP + ROWS]
        grad_v[...] += back * mixes[16 + h : 17 + h]
        talk_s[16 + h : 17 + h, :] = row_sum(back * three_s[2, 0:ROWS])
    grad_q = dot(all_keys[...], all_grad[...].reshape(HEADS * DP, DP)).T[0:ROWS]
    talk_before_grad = dot(talk_s[0:12, :], own_t, precision=HIGHEST) * (head_row * HD ** (-0.5))
    talk_after_grad = dot(own_t, talk_s[16:28, :], ((0,), (1,)), precision=HIGHEST) * head_row
    projected_s[:, :D] = grad_q
    projected_s[:, D : 2 * D] = grad_k[:, :D]
    projected_s[:, 2 * D :] = (grad_v[...] * value_mask)[:, :D]
    grad_projected = projected_s[...].astype(bf16)
    grad_normed_one = dot(grad_projected, qkv[...], NT)
    normed_one_t = (hat_one * norm_gain[...] + norm_bias[...]).T.astype(bf16)
    grad_norm_gain = row_sum(grad_normed_one * hat_one)
    grad_norm_bias = row_sum(grad_normed_one)
    handed_grad = grad_middle + norm_backward(grad_normed_one, hat_one, rs_one, norm_gain[...])
    narrow_into(handed_grad_out, handed_grad)

    talk_s[...] = jnp.zeros_like(talk_s)
    talk_s[0:12, 0:HEADS] = talk_before_grad
    talk_s[16:28, 0:HEADS] = talk_after_grad
    grad_qkv = jnp.concatenate([dot(normed_one_t, grad_projected), jnp.zeros((D, QP - 3 * D), f32)], axis=1)
    for b in range(QB - 1):
        extra = talk_s[8 * b : 8 * b + 8, 0:LANES] if b < 4 else jnp.zeros((8, LANES), f32)
        put_block(tiles_out, QKV + b, block_of(grad_qkv, b), extra)
    talk_s[0:8, :] = jnp.zeros((8, DP), f32)
    talk_s[0:1, :D] = grad_norm_gain
    talk_s[1:2, :D] = grad_norm_bias
    talk_s[2:3, :D] = grad_output_bias
    talk_s[3:4, :D] = grad_mlp_gain
    talk_s[4:5, :D] = grad_mlp_bias
    talk_s[5:6, :D] = grad_return_bias
    leading = lax.axis_index("pipe") == 0
    centred_low = centred_tokens.astype(bf16)
    centred_t = centred_tokens.T.astype(bf16)
    covariance = dot(centred_t, centred_low)
    over = iota((D, D), 0) - iota((D, D), 1)
    over = jnp.where(leading, over, -over)
    talk_s[6:7, :D] = jnp.where(leading, 0.0, row_sum(jnp.where(over == 0, covariance, 0.0)))
    wanted = (over < 0) | ((over == 0) & leading)
    covariance = jnp.concatenate([jnp.where(wanted, covariance, 0.0), jnp.zeros((D, DP - D), f32)], axis=1)
    for b in range(DB):
        put_block(tiles_out, COVARIANCE + b, block_of(covariance, b), jnp.zeros((8, LANES), f32))
    for b in range(DB):
        piece = jnp.concatenate([grad_output, jnp.zeros((D, DP - D), f32)], axis=1)
        extra = talk_s[0:8, :]
        put_block(tiles_out, OUTPUT + b, block_of(piece, b), block_of(extra, b))
    add_tail(tiles_out, QKV_TAIL, block_of(grad_qkv, QB - 1), jnp.zeros((8, LANES), f32))

    back_low = handed_grad.astype(bf16)
    handed_low_out[...] = back_low
    deep_grad[:, E - E % LANES :] = jnp.zeros((ROWS, EP - E + E % LANES), f32)
    deep_grad[:, :E] = dot(back_low, project_t[...])

    excited = wide_e[13:14, :E]
    grad_excited = row_sum(deep_grad[:, :E] * deep_s[:, :E])
    grad_excite_pre = grad_excited * excited * (1.0 - excited)
    grad_squeezed = vector_times(grad_excite_pre, excite[...], NT)
    grad_squeeze_pre = grad_squeezed * (squeeze_gate * (1.0 + squeeze_pre * (1.0 - squeeze_gate)))
    grad_pooled = vector_times(grad_squeeze_pre, squeeze_t[...], ((1,), (0,)))
    factors_out[...] = jnp.zeros_like(factors_out)

    def put_factor(start, row):
        width = row.shape[-1]
        for b in range(-(-width // LANES)):
            end = min(width, (b + 1) * LANES)
            factors_out[start + b : start + b + 1, 0 : end - b * LANES] = row[:, b * LANES : end]

    put_factor(0, wide_e[14:15, :E])
    put_factor(EB, grad_excite_pre)
    put_factor(2 * EB, squeezed)
    put_factor(2 * EB + 3, grad_squeeze_pre)
    wide_e[14:15, :E] = grad_pooled / pixels
    tail_e[...] = jnp.zeros_like(tail_e)
    batch_out[...] = jnp.zeros_like(batch_out)

    def backward_one(c, carry):
        at = pl.ds(c * LANES, LANES)
        grad_deep = (deep_grad[:, at] * wide_e[13:14, at] + wide_e[14:15, at]) * live[...]
        three = sideways(beside.at[c % 3], grad_deep)
        taps = depthwise_kernel_grad(three, active_e[:, at])
        for t in range(8):
            smalls_e[t : t + 1, at] = taps[t] * wide_e[3:4, at]
        flipped = [wide_e[12 - t : 13 - t, at] for t in range(9)]
        grad_normed = depthwise(three, flipped) * slope_e[:, at]
        centred = expanded_s[:, at] - wide_e[0:1, at]
        grad_gain = row_sum(grad_normed * centred) * wide_e[15:16, at]
        grad_bias = row_sum(grad_normed)
        batch_out[c : c + 1, :] = grad_gain
        batch_out[EB + c : EB + c + 1, :] = grad_bias
        tail_e[0:1, at] = grad_gain
        tail_e[1:2, at] = grad_bias
        tail_e[2:3, at] = taps[8] * wide_e[3:4, at]
        grad_second = grad_gain * wide_e[15:16, at] * wide_e[1:2, at] * (-1.0 / count)
        tail_e[3:4, at] = jnp.where(leading, grad_second, 0.0)
        tail_e[4:5, at] = jnp.where(leading, 0.0, grad_second)
        expanded_grad_out[:, at] = (grad_normed * wide_e[1:2, at]).astype(bf16)
        return carry

    for c in range(EB):
        backward_one(c, 0)
    grad_project = dot(handed_grad.T.astype(bf16), scaled_s[...])
    for b in range(EB - 1):
        put_block(tiles_out, PROJECT + b, block_of(grad_project, b), smalls_e[:, b * LANES : (b + 1) * LANES])
    add_tail(tiles_out, PROJECT_TAIL, block_of(grad_project, EB - 1), smalls_e[:, EP - LANES :])
    grad_expand = dot(centred_t, expanded_grad_out[...])
    for b in range(EB - 1):
        put_block(tiles_out, EXPAND + b, block_of(grad_expand, b), tail_e[:, b * LANES : (b + 1) * LANES])
    add_tail(tiles_out, EXPAND_TAIL, block_of(grad_expand, EB - 1), tail_e[:, EP - LANES :])
    spare = tiles_out.shape[0] - ALL_TILES
    if spare:
        tiles_out[ALL_TILES:] = jnp.zeros((spare, 16, LANES), bf16)

    half = pieces // 2
    fourth = half // 2
    mine = lax.axis_index("pipe")
    base = 0
    for part, order in enumerate(orders):
        size = per_piece[part]
        me = home_of(order) & (half - 1)
        for place in range(half):
            first = 2 * base + (place ^ me) * size
            start = base // 2 + (place % fourth) * size
            to = slice(start, start + size)
            kept = kept_low if place < fourth else kept_high
            sent = sent_low if place < fourth else sent_high
            kept[to] = tiles_out[pl.ds(first + mine * half * size, size)]
            sent[to] = tiles_out[pl.ds(first + (1 - mine) * half * size, size)]
        base += half * size


RIDE_ROWS = 24
RIDE_TILES = 2 * RIDE_ROWS // 16


def ridden_sum(batch, arrivals):
    total = batch[...]
    for ref in arrivals:
        end = ref.shape[0]
        both = ref[end - RIDE_TILES : end].reshape(2 * RIDE_ROWS, LANES).astype(f32)
        total = total + (both[:RIDE_ROWS] + both[RIDE_ROWS:])
    return total


def put_ride(ref, total):
    high = total.astype(bf16).astype(f32)
    both = jnp.concatenate([high, total - high], axis=0)
    end = ref.shape[0]
    ref[end - RIDE_TILES : end] = both.astype(bf16).reshape(RIDE_TILES, 16, LANES)


def added(terms, at):
    return functools.reduce(jnp.add, [term[at].astype(f32) for term in terms]).astype(bf16)


def slices_kernel(lengths, rides, *refs):
    own, other, *refs = refs
    if rides:
        batch, *refs = refs
        put_ride(refs[RIDDEN], batch[...])
    start = 0
    for length, out in zip(lengths, refs):
        out[0:length] = added([own, other], slice(start, start + length))
        start += length


def halves_kernel(count, size, rides, *refs):
    if rides:
        own, other, batch, kept, sent, batch_out = refs
        total = ridden_sum(batch, [other] if other.shape[0] > 2 * count * size else [])
        batch_out[...] = total.reshape(batch_out.shape)
        put_ride(sent, total)
    else:
        own, other, kept, sent = refs
    for i in range(count):
        here = slice(i * size, (i + 1) * size)
        there = slice((count + i) * size, (count + i + 1) * size)
        kept[here] = added([own, other], here)
        sent[here] = added([own, other], there)


def pieces_kernel(count, rows, sizes, terms_of, *refs):
    terms = []
    refs = list(refs)
    for number in terms_of:
        terms.append([refs.pop(0) for _ in range(number)])
    batch = refs.pop(0)
    batch_out = refs.pop()
    whole = count * rows * sizes[-1]
    total = ridden_sum(batch, [ref for ref in terms[-1] if ref.shape[0] > whole])
    batch_out[...] = total.reshape(batch_out.shape)
    for j, out in enumerate(refs):
        if j:
            put_ride(out, total)
        for i in range(rows):
            at = i * sum(sizes)
            for part, size in zip(terms, sizes):
                out[at : at + size] = added(part, slice((j * rows + i) * size, (j * rows + i + 1) * size))
                at += size


def finish_kernel(own, *refs):
    *others, batch, factors, held, batch_out = refs
    size = own.shape[0]
    batch_out[...] = ridden_sum(batch, others).reshape(batch_out.shape)
    held[0:size] = added([own, *others], slice(0, size))
    held[size:] = factors[...].astype(bf16).reshape(FACTOR_ROWS // 16, 16, LANES)


def side_by_side_kernel(sizes, *refs):
    outs = refs[len(refs) - len(sizes) :]
    rows = 0
    for ref in refs[: len(refs) - len(sizes)]:
        count = ref.shape[0] // sum(sizes)
        for i in range(count):
            at = i * sum(sizes)
            for out, size in zip(outs, sizes):
                out[rows * size : (rows + 1) * size] = ref[at : at + size]
                at += size
            rows += 1


def last_kernel(
    images_total, codes, sums, total, gain, tokens, handed_low, expanded_grad, expand, grad_out, wide
):
    side = code_of(codes)[0]
    count = images_total * (side * side).astype(f32)
    average, inverse = moments(sums[...], count)
    scale = inverse * gain[...]
    for b in range(EB):
        wide[0:1, b * LANES : (b + 1) * LANES] = total[b : b + 1, :]
        wide[1:2, b * LANES : (b + 1) * LANES] = total[EB + b : EB + b + 1, :]
    grad_variance = -0.5 * inverse * scale * wide[0:1, :E]
    grad_second = grad_variance / count
    grad_first = (-scale * wide[1:2, :E] - 2.0 * average * grad_variance) / count
    expanded = dot(tokens[...], expand[...])
    grad = (expanded_grad[:, :E].astype(f32) + grad_first + 2.0 * expanded * grad_second).astype(bf16)
    grad_tokens = (handed_low[...].astype(f32) + dot(grad, expand[...], NT)) * grid_mask((ROWS, D), side)
    narrow_into(grad_out, grad_tokens)


def unpack_kernel(pieces, per_piece, orders, merged, *refs):
    expand, *refs = refs
    single = (len(refs) - UNPACKED - merged) // PARTS
    inputs = refs[: merged + PARTS * single]
    (
        expand_out,
        gain_out,
        bias_out,
        depth_one_out,
        squeeze_out,
        squeeze_bias_out,
        excite_out,
        excite_bias_out,
        project_out,
        norm_gain_out,
        norm_bias_out,
        qkv_out,
        talk_before_out,
        talk_after_out,
        output_out,
        output_bias_out,
        mlp_gain_out,
        mlp_bias_out,
        hidden_out,
        hidden_bias_out,
        depth_two_out,
        return_out,
        return_bias_out,
        tiles,
        factors,
        wide,
    ) = refs[merged + PARTS * single :]
    for part, order in enumerate(orders):
        me = home_of(order)
        size = per_piece[part]
        base = sum(per_piece[:part])
        at = 0
        riding = FACTOR_ROWS // 16
        own = inputs[merged + part * single : merged + (part + 1) * single]
        for number, ref in enumerate(inputs[:merged] + own):
            width = sum(per_piece) + riding if number < merged else size + riding * (part == RIDDEN)
            skipped = base if number < merged else 0
            for inner in range(ref.shape[0] // width):
                home = at ^ me
                start = inner * width + skipped
                tiles[pl.ds(base * pieces + home * size, size)] = ref[start : start + size]
                if part == RIDDEN:
                    factor = ref[start + size : start + size + riding]
                    factors[home] = factor.reshape(FACTOR_ROWS, LANES).astype(f32)
                at += 1

    def block(b):
        return tiles[b * TILES : (b + 1) * TILES].reshape(ROWS, LANES).astype(f32)

    def spread(first, count, width, out, take, tail=None):
        for b in range(count):
            value = block(first + b) if b < count - 1 or tail is None else pltpu.roll(block(tail), LANES - TAIL_LANE, 1)
            start, stop = b * LANES, min(width, (b + 1) * LANES)
            out[:, start:stop] = value[0:D, 0 : stop - start]
            for ref, top, row, rows in take:
                if len(ref.shape) == 1:
                    ref[start:stop] = value[D + row, 0 : stop - start]
                else:
                    ref[top : top + rows, start:stop] = value[D + row : D + row + rows, 0 : stop - start]

    spread(PROJECT, EB, E, project_out, [(depth_one_out, 0, 0, 8)], PROJECT_TAIL)
    spread(HIDDEN, FB, F, hidden_out, [(depth_two_out, 0, 0, 8)])
    spread(RETURN, FB, F, return_out, [(depth_two_out, 8, 0, 1), (hidden_bias_out, 0, 1, 1)])
    spread(QKV, QB, 3 * D, qkv_out, [], QKV_TAIL)

    def gathered(start, width):
        columns = [factors[:, start + b, :] for b in range(-(-width // LANES))]
        return jnp.concatenate(columns, axis=1)[:, 0:width]

    pooled = gathered(0, E)
    grad_excite_pre = gathered(EB, E)
    squeezed = gathered(2 * EB, SQ)
    grad_squeeze_pre = gathered(2 * EB + 3, SQ)
    squeeze_out[...] = dot(grad_squeeze_pre.T.astype(bf16), pooled.astype(bf16))
    excite_out[...] = dot(squeezed.T.astype(bf16), grad_excite_pre.astype(bf16))
    squeeze_bias_out[...] = jnp.sum(grad_squeeze_pre, axis=0)
    excite_bias_out[...] = jnp.sum(grad_excite_pre, axis=0)

    tail = pltpu.roll(block(EXPAND_TAIL), LANES - TAIL_LANE, 1)
    for b in range(EB):
        value = block(EXPAND + b) if b < EB - 1 else tail
        wide[:, b * LANES : (b + 1) * LANES] = value
    gain_out[...] = wide[D, 0:E]
    bias_out[...] = wide[D + 1, 0:E]
    depth_one_out[8:9, :] = wide[D + 2 : D + 3, 0:E]
    both = jnp.concatenate([block(COVARIANCE), block(COVARIANCE + 1)], axis=1)[0:D, 0:D]
    turned = both.T
    over = iota((D, D), 0) - iota((D, D), 1)
    diagonal = jnp.concatenate([block(OUTPUT)[D + 6 : D + 7], block(OUTPUT + 1)[D + 6 : D + 7]], axis=1)[:, 0:D]
    first = jnp.where(over <= 0, both, turned).astype(bf16)
    second = jnp.where(over > 0, both, jnp.where(over < 0, turned, diagonal)).astype(bf16)
    added = dot(first, expand[...]) * wide[D + 3 : D + 4, 0:E] + dot(second, expand[...]) * wide[D + 4 : D + 5, 0:E]
    expand_out[...] = wide[0:D, 0:E] + added
    vectors = (norm_gain_out, norm_bias_out, output_bias_out, mlp_gain_out, mlp_bias_out, return_bias_out)
    spread(OUTPUT, DB, D, output_out, [(ref, 0, row, 1) for row, ref in enumerate(vectors)])
    talk_before_out[0:8] = block(QKV)[D : D + 8, 0:HEADS]
    talk_before_out[8:12] = block(QKV + 1)[D : D + 4, 0:HEADS]
    talk_after_out[0:8] = block(QKV + 2)[D : D + 8, 0:HEADS]
    talk_after_out[8:12] = block(QKV + 3)[D : D + 4, 0:HEADS]

def kernel_call(body, name, shapes, scratch, operands, fetched, limit, flops):
    in_specs = [pl.BlockSpec(memory_space=pltpu.VMEM)] * len(operands)
    if fetched is not None:
        if operands[0].dtype == jnp.int32:
            in_specs[0] = pl.BlockSpec(memory_space=pltpu.SMEM)
        in_specs += [pl.BlockSpec(memory_space=pltpu.HBM)] * len(fetched)
    return pl.pallas_call(
        body,
        out_shape=[jax.ShapeDtypeStruct(shape, kind) for shape, kind in shapes],
        in_specs=in_specs,
        out_specs=[pl.BlockSpec(memory_space=pltpu.VMEM)] * len(shapes),
        scratch_shapes=scratch,
        compiler_params=pltpu.CompilerParams(vmem_limit_bytes=limit * MIB),
        cost_estimate=pl.CostEstimate(flops=flops, bytes_accessed=8 * MIB, transcendentals=0),
        name=name,
    )(*operands, *(fetched or ()))


def swapped(value, axis, mask):
    size = lax.axis_size(axis)
    return lax.ppermute(value, axis, [(i, i ^ mask) for i in range(size)])


def summed_over_dp(value, bits):
    for first in range(0, bits, 2):
        here = [1 << b for b in range(first, min(first + 2, bits))]
        masks = here + ([here[0] | here[1]] if len(here) == 2 else [])
        others = [swapped(value, "dp", mask) for mask in masks]
        value = value + functools.reduce(jnp.add, others)
    return value


def on_device(
    images,
    codes,
    cotangent,
    expand_weight,
    batch_gain,
    batch_bias,
    depth_one,
    squeeze_weight,
    squeeze_bias,
    excite_weight,
    excite_bias,
    project_weight,
    norm_gain,
    norm_bias,
    qkv_weight,
    talk_before,
    talk_after,
    output_weight,
    output_bias,
    mlp_gain,
    mlp_bias,
    hidden_weight,
    hidden_bias,
    depth_two,
    return_weight,
    return_bias,
):
    devices_dp = lax.axis_size("dp")
    bits = devices_dp.bit_length() - 1
    pieces = 2 * devices_dp
    half = pieces // 2
    images_total = float(images.shape[1] * devices_dp)
    per_piece = -(-ALL_TILES // pieces)
    per_piece = [per_piece - per_piece // 2, per_piece // 2]
    factor_tiles = FACTOR_ROWS // 16
    pipe = lax.axis_index("pipe")

    rest = list(range(2, bits))
    groups = [rest[g : g + 2] for g in range(0, len(rest), 2)]
    orders = [[1, 0] + rest, [0, 1] + rest]
    image = lax.dynamic_index_in_dim(images, pipe, 0, keepdims=False)[0]
    upstream = lax.dynamic_index_in_dim(cotangent, pipe, 0, keepdims=False)[0]

    def row(vector):
        return vector.reshape(1, -1)

    def buffers(arrays):
        return [pltpu.VMEM(a.shape, a.dtype) for a in arrays]

    squeeze_t = squeeze_weight.T
    project_t = project_weight.T
    return_t = return_weight.T
    gain = row(batch_gain)

    sums, tokens, expanded = kernel_call(
        sums_kernel,
        "sums",
        [((3, E), f32), ((ROWS, D), bf16), ((ROWS, EP), f32)],
        buffers([expand_weight]) + [pltpu.SMEM(codes.shape, codes.dtype), pltpu.SemaphoreType.DMA((2,))],
        (image,),
        (expand_weight, codes),
        16,
        1 << 33,
    )
    sums = summed_over_dp(sums, bits)

    operands = (
        codes,
        tokens,
        expanded,
        upstream,
        sums,
        gain,
        row(batch_bias),
        row(squeeze_bias),
        row(excite_bias),
        row(hidden_bias),
        depth_one,
        squeeze_t,
        excite_weight,
        project_t,
        row(norm_gain),
        row(norm_bias),
        qkv_weight,
        talk_before,
        talk_after,
        output_weight,
        row(output_bias),
        row(mlp_gain),
        row(mlp_bias),
        hidden_weight,
        depth_two,
        return_t,
        row(return_bias),
    )
    shapes = [
        ((PIX, D), bf16),
        ((PIX, D), bf16),
        ((PIX, D), f32),
        ((ROWS, D), bf16),
        ((ROWS, EP), bf16),
        ((RIDE_ROWS, LANES), f32),
        *[((sum(per_piece) * half // 2, 16, LANES), bf16)] * 4,
        ((FACTOR_ROWS, LANES), f32),
    ]
    scratch = [
        pltpu.VMEM((sum(per_piece) * pieces, 16, LANES), bf16),
        pltpu.VMEM((16, EP), f32),
        pltpu.VMEM((16, FP), f32),
        pltpu.VMEM((ROWS, LANES), f32),
        pltpu.VMEM((ROWS, LANES), f32),
        pltpu.VMEM((3, ROWS + 16, LANES), f32),
        pltpu.VMEM((8, EP), f32),
        pltpu.VMEM((ROWS, EP), f32),
        pltpu.VMEM((ROWS, EP), f32),
        pltpu.VMEM((ROWS, EP), f32),
        pltpu.VMEM((ROWS, EP), f32),
        pltpu.VMEM((ROWS, EP), bf16),
        pltpu.VMEM((32, DP), f32),
        pltpu.VMEM((3, DP, DP), f32),
        pltpu.VMEM((ROWS, DP), f32),
        pltpu.VMEM((HEADS, ROWS, DP), f32),
        pltpu.VMEM((HEADS, DP, DP), bf16),
        pltpu.VMEM((HEADS, DP, DP), bf16),
        pltpu.VMEM((D, HEADS * DP), bf16),
        pltpu.VMEM((D, HEADS * DP), bf16),
        pltpu.VMEM((ROWS, FP), f32),
        pltpu.VMEM((ROWS, FP), f32),
        pltpu.VMEM((ROWS, FP), bf16),
        pltpu.VMEM((ROWS, FP), bf16),
        pltpu.VMEM((ROWS, FP), f32),
        pltpu.VMEM((8, EP), f32),
        pltpu.VMEM((8, EP), f32),
        pltpu.VMEM((16, FP), f32),
        pltpu.VMEM((ROWS, DP), f32),
        pltpu.VMEM((ROWS, DP), f32),
        pltpu.VMEM((32, DP), f32),
        pltpu.VMEM((ROWS, 3 * D), f32),
    ]
    first, second, handed_grad, handed_low, expanded_grad, batch, *packed, factors = kernel_call(
        functools.partial(middle_kernel, images_total, pieces, per_piece, orders),
        "middle",
        shapes,
        scratch,
        operands,
        (),
        40,
        1 << 32,
    )

    def masks_of(group):
        return [sum(1 << b for i, b in enumerate(group) if (j >> (len(group) - 1 - i)) & 1) for j in range(1 << len(group))]

    def tiles_of(count):
        return ((count, 16, LANES), bf16)

    def small_kernel(body, name, shapes, operands):
        return kernel_call(body, name, shapes, [], operands, None, 2, 1 << 20)

    kept_low, kept_high, sent_low, sent_high = packed
    arrived_high = swapped(sent_high, "pipe", 1)
    arrived_low = swapped(sent_low, "pipe", 1)
    count = half // 2
    lengths = [count * size for size in per_piece]
    riding = [length + RIDE_TILES * (part == RIDDEN) for part, length in enumerate(lengths)]
    going = small_kernel(
        functools.partial(slices_kernel, lengths, True),
        "firsts",
        [tiles_of(length) for length in riding],
        (kept_high, arrived_high, batch),
    )
    arrived = [swapped(value, "dp", 1 << order[0]) for value, order in zip(going, orders)]
    mine = small_kernel(
        functools.partial(slices_kernel, lengths, False),
        "keeps",
        [tiles_of(length) for length in lengths],
        (kept_low, arrived_low),
    )
    terms = [list(pair) for pair in zip(mine, arrived)]
    held = [None] * PARTS
    count //= 2
    for part, order in enumerate(orders):
        size = per_piece[part]
        rides = part == RIDDEN
        body = functools.partial(halves_kernel, count, size, rides)
        shapes = [tiles_of(count * size), tiles_of(count * size + RIDE_TILES * rides)]
        if rides:
            mine, going, batch = small_kernel(body, "halves", shapes + [((RIDE_ROWS, LANES), f32)], (*terms[part], batch))
        else:
            mine, going = small_kernel(body, "halves", shapes, terms[part])
        held[part] = (mine, swapped(going, "dp", 1 << order[1]))
    terms = [list(pair) for pair in held]
    sizes = per_piece
    for group in groups:
        masks = masks_of(group)
        count //= len(masks)
        body = functools.partial(pieces_kernel, len(masks), count, sizes, [len(part) for part in terms])
        shapes = [tiles_of(count * sum(sizes) + (RIDE_TILES if j else 0)) for j in range(len(masks))]
        *going, batch = small_kernel(
            body, "pieces", shapes + [((RIDE_ROWS, LANES), f32)], (*[term for part in terms for term in part], batch)
        )
        sizes = [sum(sizes)]
        terms = [[going[0]] + [swapped(value, "dp", mask) for value, mask in zip(going[1:], masks[1:])]]
    held, batch = small_kernel(
        finish_kernel, "finish", [tiles_of(sum(sizes) + factor_tiles), ((RIDE_ROWS, LANES), f32)], (*terms[0], batch, factors)
    )
    (images_grad,) = kernel_call(
        functools.partial(last_kernel, images_total),
        "last",
        [((PIX, D), f32)],
        [pltpu.VMEM((2, EP), f32)],
        (codes, sums, batch, gain, tokens, handed_low, expanded_grad, expand_weight),
        (),
        16,
        1 << 31,
    )

    sizes = [per_piece[0], per_piece[1] + factor_tiles]
    merged = [held]
    for number, group in enumerate(reversed(groups)):
        merged += [swapped(held, "dp", mask) for mask in masks_of(group)[1:]]
        count *= 1 << len(group)
        if number < len(groups) - 1:
            (held,) = small_kernel(
                functools.partial(side_by_side_kernel, [sum(sizes)]), "together", [tiles_of(count * sum(sizes))], merged
            )
    held = list(
        small_kernel(
            functools.partial(side_by_side_kernel, sizes), "apart", [tiles_of(count * size) for size in sizes], merged
        )
    )
    held, images_grad = lax.optimization_barrier((held, images_grad))
    held = list(held)

    leading = pipe == 0

    def both_layers(one, two):
        other = swapped(jnp.where(leading, two, one), "pipe", 1)
        return jnp.where(leading, jnp.stack([one, other]), jnp.stack([other, two]))[None, :, None]

    activations = with_layout_constraint(both_layers(first, second), Layout(major_to_minor=(0, 2, 3, 1, 4)))
    input_grads = with_layout_constraint(
        both_layers(images_grad, handed_grad), Layout(major_to_minor=(0, 1, 3, 2, 4))
    )
    collected = [[], []]
    across = [[], []]
    for step in (1, 0):
        arrived = [swapped(value, "dp", 1 << order[step]) for value, order in zip(held[::-1], orders[::-1])][::-1]
        for part, size in enumerate(sizes):
            collected[part].append(arrived[part])
            if step:
                (held[part],) = small_kernel(
                    functools.partial(side_by_side_kernel, [size]),
                    "together",
                    [tiles_of(2 * count * size)],
                    (held[part], arrived[part]),
                )
        if step:
            across = [[swapped(value, "pipe", 1)] for value in held]
        else:
            arrived, activations, input_grads = lax.optimization_barrier((arrived, activations, input_grads))
            across = [early + [swapped(value, "pipe", 1)] for early, value in zip(across, arrived)]
    collected = [own + other for own, other in zip(collected, across)]
    grads = kernel_call(
        functools.partial(unpack_kernel, pieces, per_piece, orders, len(merged)),
        "unpack",
        [
            ((D, E), f32),
            ((E,), f32),
            ((E,), f32),
            ((9, E), f32),
            ((SQ, E), f32),
            ((SQ,), f32),
            ((SQ, E), f32),
            ((E,), f32),
            ((D, E), f32),
            ((D,), f32),
            ((D,), f32),
            ((D, 3 * D), f32),
            ((HEADS, HEADS), f32),
            ((HEADS, HEADS), f32),
            ((D, D), f32),
            ((D,), f32),
            ((D,), f32),
            ((D,), f32),
            ((D, F), f32),
            ((F,), f32),
            ((9, F), f32),
            ((D, F), f32),
            ((D,), f32),
        ],
        [
            pltpu.VMEM((sum(per_piece) * pieces, 16, LANES), bf16),
            pltpu.VMEM((pieces, FACTOR_ROWS, LANES), f32),
            pltpu.VMEM((ROWS, EP), f32),
        ],
        (expand_weight, *merged, *collected[0], *collected[1]),
        None,
        40,
        1 << 26,
    )
    grads = list(grads)
    for transposed in (4, 8, 21):
        grads[transposed] = grads[transposed].T

    return (activations, input_grads, *grads)


def solution(mesh):
    in_specs = (P(None, "dp", None, None), P(), P(None, "dp", None, None)) + (P(),) * 23
    out_specs = (P("pipe", None, "dp", None, None), P("pipe", None, "dp", None, None)) + (P(),) * 23
    return jax.shard_map(on_device, mesh=mesh, in_specs=in_specs, out_specs=out_specs, check_vma=False)
```
